32 devices in a mesh: dict: 4 (over z), scan: 8 (over y, x, core).
Axes of the slice: x: 2, y: 2, z: 4, core: 2. Of those that a mesh axis runs over, the one named last changes fastest.
Arguments:
- patterns: float32 [128, 64, 3600], P('scan', 'dict'), may hold values from -63 to 63
- background: float32 [3600], replicated, may hold values from -6 to 6
- templates: bfloat16 [512, 3600], P('dict'), may hold values from -19.5 to 19.5
- grain_id: int32 [128, 64], P('scan', 'dict'), may hold values from 0 to 31
- keep_mask: int32 [128, 64], P('scan', 'dict'), may hold values 0 or 1
- grain_row: int32 [32], replicated, may hold values from 0 to 31, each once
Outputs:
- max_score: float32 [128, 64], P('scan', 'dict')
- grain_patterns: float32 [32, 3600], P('scan')
The draws below stay inside these ranges and needn't reach their ends.
Inputs may be any that keep to these rules, and one draw needn't show every extreme that they name: grain_row holds each of 0 to 31 once.
All inputs are finite; a program needn't handle non-finite values. No bound on the sum of `keep_mask` on one device may be relied on, other than what follows from the above.
Results may differ from the reference program's by a relative error of at most 0.0045.
Values may be sent and summed in bfloat16 or wider, within the bound.
A program may use at most 128 MiB of HBM per device.

```python
import math
import jax
import jax.numpy as jnp
import numpy as np
from jax import lax

PIX = 3600
SCAN_ROWS = 128
SCAN_COLS = 64
TEMPLATES = 512
GRAINS = 32


def draw_patterns(key, part):
    noise_key = jax.random.fold_in(key, 11)
    scale_key = jax.random.fold_in(key, 12)
    shift_key = jax.random.fold_in(key, 13)
    full_shape = (SCAN_ROWS, SCAN_COLS, PIX)
    point_shape = (SCAN_ROWS, SCAN_COLS, 1)
    values_raw = jnp.clip(jax.random.normal(noise_key, full_shape, jnp.float32), -6.0, 6.0)
    spread = jnp.exp(jax.random.uniform(scale_key, point_shape, jnp.float32, 0.0, math.log(10.0)))
    offset = jax.random.uniform(shift_key, point_shape, jnp.float32, -3.0, 3.0)
    return values_raw * spread + offset


def draw_templates(key, part):
    noise_key = jax.random.fold_in(key, 21)
    scale_key = jax.random.fold_in(key, 22)
    shift_key = jax.random.fold_in(key, 23)
    full_shape = (TEMPLATES, PIX)
    template_shape = (TEMPLATES, 1)
    values_raw = jnp.clip(jax.random.normal(noise_key, full_shape, jnp.float32), -6.0, 6.0)
    spread = jnp.exp(jax.random.uniform(scale_key, template_shape, jnp.float32, math.log(0.3), math.log(3.0)))
    offset = jax.random.uniform(shift_key, template_shape, jnp.float32, -1.5, 1.5)
    return (values_raw * spread + offset).astype(jnp.bfloat16)


def with_ends(drawn, rng, smallest, largest):
    shape = drawn.shape
    place = [jax.random.randint(jax.random.fold_in(rng, axis), (), 0, shape[axis]) for axis in range(len(shape))]
    drawn = drawn.at[tuple(place)].set(smallest)
    longest = shape.index(max(shape))
    place[longest] = (place[longest] + 1) % shape[longest]
    return drawn.at[tuple(place)].set(largest)


def rank_bounds(amount, lean):
    loads = [(1 << 20) // math.isqrt(rank ** lean) + 1 for rank in range(1, amount + 1)]
    scale = 1 + sum(loads) // (1 << 30)
    return np.cumsum(np.array([max(1, weight // scale) for weight in loads]))


def skewed_ids(stream_key, shape, amount, skew):
    table = rank_bounds(amount, skew)
    ticket = jax.random.randint(jax.random.fold_in(stream_key, 1), shape, 0, int(table[amount - 1]))
    standing = jnp.searchsorted(jnp.asarray(table, jnp.int32), ticket, side="right")
    return jax.random.permutation(jax.random.fold_in(stream_key, 2), amount)[standing].astype(jnp.int32)


def scatter_about(rng, dims, deviation, limit, held_as=jnp.bfloat16):
    entries = jax.random.normal(rng, dims, jnp.float32) * deviation
    return jnp.minimum(jnp.maximum(entries, -limit), limit).astype(held_as)


def setup_inputs(seed: int = 0) -> dict:
    key_of = jax.random.split(jax.random.key(seed), 7)
    return {
        "patterns": draw_patterns(jax.random.fold_in(key_of[6], 71), 0),
        "background": scatter_about(key_of[1], (PIX,), 1.0, 6.0, jnp.float32),
        "templates": draw_templates(jax.random.fold_in(key_of[6], 71), 0),
        "grain_id": with_ends(skewed_ids(key_of[3], (SCAN_ROWS, SCAN_COLS), GRAINS, 2), jax.random.fold_in(key_of[3], 3), 0, GRAINS - 1).astype(jnp.int32),
        "keep_mask": with_ends((jax.random.randint(key_of[4], (SCAN_ROWS, SCAN_COLS), 0, 4) < 3).astype(jnp.int32), jax.random.fold_in(key_of[4], 1), 0, 1),
        "grain_row": jax.random.permutation(key_of[5], GRAINS).astype(jnp.int32),
    }


def unit_rows(values):
    mean_square = lax.optimization_barrier(jnp.mean(values * values, axis=-1, keepdims=True))
    return values * lax.rsqrt(mean_square + 1e-05)

def filter_points(measured, background):
    centered = measured - background
    centered = centered - lax.optimization_barrier(jnp.mean(centered, axis=-1, keepdims=True))
    return unit_rows(centered).astype(jnp.bfloat16)

def reference(patterns, background, templates, grain_id, keep_mask, grain_row):

    def filter_one(measured_row):
        return filter_points(measured_row, background)
    filtered = lax.map(filter_one, patterns)
    padded = jnp.pad(filtered, ((1, 1), (1, 1), (0, 0)))
    centered_panel = templates.astype(jnp.float32)
    centered_panel = centered_panel - lax.optimization_barrier(jnp.mean(centered_panel, axis=-1, keepdims=True))
    unit_panel = unit_rows(centered_panel).astype(jnp.bfloat16)
    grain_index = jnp.arange(GRAINS, dtype=jnp.int32)
    point_rows = lax.optimization_barrier(jnp.sum(jnp.where(grain_id[:, :, None] == grain_index, grain_row, 0), axis=2)).astype(jnp.int32)
    root_inverse = 1.0 / math.sqrt(PIX)

    def one_row(totals, row_number):
        row_block = lax.dynamic_slice_in_dim(padded, row_number, 3, 0)
        neighbour = jnp.zeros((SCAN_COLS, PIX), jnp.float32)
        for row_shift in range(3):
            for col_shift in range(3):
                neighbour = neighbour + row_block[row_shift, col_shift:col_shift + SCAN_COLS].astype(jnp.float32)
        indexed = unit_rows(neighbour).astype(jnp.bfloat16)
        scores = lax.dot_general(indexed, unit_panel, (((1,), (1,)), ((), ())), preferred_element_type=jnp.float32)
        best_row = lax.optimization_barrier(jnp.max(scores, axis=1)) * root_inverse
        row_of_points = lax.dynamic_index_in_dim(point_rows, row_number, 0, keepdims=False)
        keep_row = lax.dynamic_index_in_dim(keep_mask, row_number, 0, keepdims=False)
        selector = ((row_of_points[:, None] == grain_index[None, :]) & (keep_row[:, None] == 1)).astype(jnp.bfloat16)
        totals = totals + lax.dot_general(selector, indexed, (((0,), (0,)), ((), ())), preferred_element_type=jnp.float32)
        return (totals, best_row)
    totals, max_score = lax.scan(one_row, jnp.zeros((GRAINS, PIX), jnp.float32), jnp.arange(SCAN_ROWS, dtype=jnp.int32))
    return (max_score, unit_rows(totals))
```

```python
import functools

import jax
import jax.numpy as jnp
from jax import lax
from jax.experimental import pallas as pl
from jax.experimental.pallas import tpu as pltpu
from jax.sharding import PartitionSpec as P

MESH = pl.DeviceIdType.MESH
EPS = 1e-05
GROUP = 8
F32 = jnp.float32
BF16 = jnp.bfloat16


def iota(shape, dim):
    return lax.broadcasted_iota(jnp.int32, shape, dim)


def near(a, b):
    return (a - b <= 1) & (b - a <= 1)


def unit(values, pixels):
    square = jnp.sum(values * values, axis=-1, keepdims=True) * (1.0 / pixels)
    return values * lax.rsqrt(square + EPS)


def centred(values, pixels):
    return values - jnp.sum(values, axis=-1, keepdims=True) * (1.0 / pixels)


def kernel(
    D, S, G, TR, TC, pix, R,
    patterns, templates, background, grain_id, keep_mask, grain_row,
    score_out, grain_out,
    pat, raw, filt, near_mat, pick_mat, halo_mat, sel_mat,
    edge, corner_src, corner_dst, halo, neigh, indexed, panel,
    gsum, grecv, zbuf, best,
    pat_sem, raw_sem, zsend, nsend, trecv, hsend, hrecv,
    gsend, grecv_sem, zgsend, zgrecv,
):
    z = lax.axis_index("dict")
    s = lax.axis_index("scan")
    points = TR * TC
    rows_out = G // S
    cuts = [(a, min(a + 512, pix)) for a in range(0, pix, 512)]

    def pat_copy(i):
        return pltpu.make_async_copy(patterns.at[i], pat.at[i], pat_sem.at[i])

    raw_copy = pltpu.make_async_copy(templates, raw, raw_sem)
    raw_copy.start()
    for i in range(TR):
        pat_copy(i).start()

    halo[...] = jnp.zeros_like(halo)

    barrier = pltpu.get_barrier_semaphore()

    def hello(zz, ss):
        pl.semaphore_signal(
            barrier, inc=1, device_id={"dict": zz, "scan": ss}, device_id_type=MESH
        )

    for k in range(1, S):
        hello(z, lax.rem(s + k, S))
    for k in range(1, D):
        hello(lax.rem(z + k, D), s)
    diagonals = [(-1, -1), (-1, 1), (1, -1), (1, 1)]

    def inside(ds, dz):
        ok = None
        for cond in (
            [s >= 1] if ds < 0 else [s <= S - 2] if ds > 0 else []
        ) + ([z >= 1] if dz < 0 else [z <= D - 2] if dz > 0 else []):
            ok = cond if ok is None else ok & cond
        return ok

    for ds, dz in diagonals:
        @pl.when(inside(ds, dz))
        def _():
            hello(z + dz, s + ds)

    p0, q1 = iota((points, points), 0), iota((points, points), 1)
    near_mat[...] = jnp.where(
        near(p0 // TC, q1 // TC) & near(p0 % TC, q1 % TC), 1.0, 0.0
    ).astype(BF16)
    i0, q = iota((48, points), 0), iota((48, points), 1)
    k0 = (i0 - 32) // 2
    corner_at = jnp.where(
        k0 == 0, 0, jnp.where(k0 == 1, TC - 1, jnp.where(k0 == 2, points - TC, points - 1))
    )
    want = jnp.where(
        i0 < 16, i0 * TC, jnp.where(i0 < 32, (i0 - 16) * TC + TC - 1,
                                    jnp.where(i0 < 40, corner_at, -1))
    )
    pick_mat[...] = jnp.where(q == want, 1.0, 0.0).astype(BF16)
    p, h = iota((points, 128), 0), iota((points, 128), 1)
    slot, i = h // 16, h % 16
    r, c = p // TC, p % TC
    side = (
        ((slot == 0) & (r == 0) & near(c, i))
        | ((slot == 1) & (r == TR - 1) & near(c, i))
        | ((slot == 2) & (c == 0) & near(r, i))
        | ((slot == 3) & (c == TC - 1) & near(r, i))
        | ((slot == 4) & (i == 0) & (p == 0))
        | ((slot == 5) & (i == 0) & (p == TC - 1))
        | ((slot == 6) & (i == 0) & (p == points - TC))
        | ((slot == 7) & (i == 0) & (p == points - 1))
    )
    halo_mat[...] = jnp.where(side, 1.0, 0.0).astype(BF16)
    code = jnp.where(keep_mask[...] == 1, grain_id[...], -1).astype(F32).astype(BF16)
    spread = jnp.where(iota((TC, points), 1) % TC == iota((TC, points), 0), 1.0, 0.0).astype(BF16)
    wide = jnp.dot(code, spread, preferred_element_type=F32)
    own = iota((TR, points), 1) // TC == iota((TR, points), 0)
    code_row = jnp.sum(jnp.where(own, wide, 0.0), axis=0, keepdims=True)
    one_hot = jnp.where(
        iota((G, points), 0).astype(F32) == code_row, 1.0, 0.0
    ).astype(BF16)
    to_row = jnp.where(iota((G, G), 0) == grain_row[...], 1.0, 0.0).astype(BF16)
    sel_mat[...] = jnp.dot(to_row, one_hot, preferred_element_type=F32).astype(BF16)

    piece = lax.rem(s, GROUP)
    base = s - piece
    core = lax.rem(piece, 2)
    xbit = lax.rem(piece // 2, 2)
    ybit = piece // 4
    px, py = piece + 2 - 4 * xbit, piece + 4 - 8 * ybit
    first = jnp.where(core == 0, px, py)
    second = jnp.where(core == 0, py, px)
    twin = 1 - 2 * core
    across = first + second - piece

    def remote(src, dst, ssem, rsem, zz, ss):
        return pltpu.make_async_remote_copy(
            src_ref=src, dst_ref=dst, send_sem=ssem, recv_sem=rsem,
            device_id={"dict": zz, "scan": ss}, device_id_type=MESH,
        )

    def shard_copy(d, q, ssem, zz, ss):
        return remote(panel.at[d, q], panel.at[d, q], ssem, trecv.at[d, q], zz, ss)

    def z_copy(d, sem_at, zz):
        return shard_copy(d, piece, zsend.at[sem_at], zz, s)

    def normalise(j):
        panel[z, j] = unit(centred(raw[j].astype(F32), pix), pix).astype(BF16)

    near_end = jnp.minimum(z, D - 1 - z)

    def event_shard(e):
        paired = e <= 2 * near_end
        k = jnp.where(paired, (e + 1) // 2, e - near_end)
        lower = jnp.where(paired, e % 2 == 1, z > near_end)
        return jnp.where(lower, z - k, z + k)

    def relay(d):
        target = jnp.where(d < z, z + 1, z - 1)
        return (target >= 0) & (target < D), target

    def piece_sends(d):
        return [
            (piece, 0, first), (piece, 1, second), (piece, 2, piece + twin),
            (first, 3, second), (first, 4, piece + twin),
            (second, 5, piece + twin), (across, 6, piece + twin),
        ]

    def in_plane(d, which):
        q, k, to = piece_sends(d)[which]
        return shard_copy(d, q, nsend.at[d, k], z, base + to)

    def arrived(d, q):
        shard_copy(d, q, nsend.at[d, 0], z, base + first).wait_recv()

    def stage_a(e):
        d = event_shard(e)
        arrived(d, piece)
        on, target = relay(d)

        @pl.when(on)
        def _():
            z_copy(d, d, target).start()

        for which in (0, 1, 2):
            in_plane(d, which).start()

    def stage_b(e):
        d = event_shard(e)
        arrived(d, first)
        for which in (3, 4):
            in_plane(d, which).start()

    def stage_c(e):
        d = event_shard(e)
        arrived(d, second)
        in_plane(d, 5).start()
        arrived(d, across)
        in_plane(d, 6).start()

    def score(d):
        dots = lax.dot_general(
            panel[d].reshape(R, pix), indexed[...], (((1,), (1,)), ((), ())),
            preferred_element_type=F32,
        )
        best[...] = jnp.maximum(best[...], jnp.max(dots, axis=0, keepdims=True))

    def stage_d(e):
        d = event_shard(e)
        for q in (piece, first, second, across):
            arrived(d, q + twin)
        score(d)

    def stage_end(e):
        d = event_shard(e)
        on, target = relay(d)

        @pl.when(on)
        def _():
            z_copy(d, d, target).wait_send()

        for which in range(7):
            in_plane(d, which).wait_send()

    halo_moves = [
        (filt.at[TR - 1], halo.at[0], 1, 0),
        (filt.at[0], halo.at[1], -1, 0),
        (edge.at[1], halo.at[2], 0, 1),
        (edge.at[0], halo.at[3], 0, -1),
        (corner_src.at[3], corner_dst.at[0], 1, 1),
        (corner_src.at[2], corner_dst.at[1], 1, -1),
        (corner_src.at[1], corner_dst.at[2], -1, 1),
        (corner_src.at[0], corner_dst.at[3], -1, -1),
    ]

    def halo_copy(k):
        src, dst, ds, dz = halo_moves[k]
        return remote(src, dst, hsend.at[k], hrecv.at[k], z + dz, s + ds)

    def halo_send(k):
        @pl.when(inside(halo_moves[k][2], halo_moves[k][3]))
        def _():
            halo_copy(k).start()

    diag_count = sum(
        [jnp.where(inside(ds, dz), 1, 0) for ds, dz in diagonals]
    )
    pl.semaphore_wait(barrier, S - 1 + D - 1 + diag_count)

    raw_copy.wait()
    normalise(piece)

    @pl.when(z < D - 1)
    def _():
        z_copy(z, z, z + 1).start()

    @pl.when(z > 0)
    def _():
        z_copy(z, D, z - 1).start()

    def filter_row(i):
        centre = centred(pat[i] - background[...], pix)
        filt[i] = unit(centre, pix).astype(BF16)

    for i in range(TR):
        pat_copy(i).wait()
    filter_row(TR - 1)
    halo_send(0)
    filter_row(0)
    halo_send(1)

    @pl.loop(1, TR - 1)
    def _(i):
        filter_row(i)

    for a, b in cuts:
        got = jnp.dot(
            pick_mat[...], filt[:, :, a:b].reshape(points, b - a), preferred_element_type=F32
        ).astype(BF16)
        edge[0, :, a:b] = got[0:16]
        edge[1, :, a:b] = got[16:32]
        for k in range(4):
            corner_src[k, :, a:b] = got[32 + 2 * k : 34 + 2 * k]
    for k in range(2, 8):
        halo_send(k)

    events = min(D - 1, 3)
    stage_a(1)

    for j in range(1, GROUP):
        normalise(lax.rem(piece + j, GROUP))

    for a, b in cuts:
        neigh[:, a:b] = jnp.dot(
            near_mat[...], filt[:, :, a:b].reshape(points, b - a), preferred_element_type=F32
        )
    stage_b(1)
    if events >= 2:
        stage_a(2)

    for k in range(8):
        ds, dz = halo_moves[k][2], halo_moves[k][3]

        @pl.when(inside(-ds, -dz))
        def _():
            halo_copy(k).wait_recv()
            if k >= 4:
                halo[k, 0:2, :] = corner_dst[k - 4]

    total = jnp.zeros((points, 1), F32)
    for a, b in cuts:
        part = neigh[:, a:b] + jnp.dot(
            halo_mat[...], halo[:, :, a:b].reshape(128, b - a), preferred_element_type=F32
        )
        neigh[:, a:b] = part
        total = total + jnp.sum(part * part, axis=1, keepdims=True)
    scale = lax.rsqrt(total * (1.0 / pix) + EPS)
    for a, b in cuts:
        indexed[:, a:b] = (neigh[:, a:b] * scale).astype(BF16)

    for a, b in cuts:
        sums = jnp.dot(sel_mat[...], indexed[:, a:b], preferred_element_type=F32).astype(BF16)
        for k in range(S):
            gsum[k, :, a:b] = sums[k * rows_out : (k + 1) * rows_out]

    def grain_copy(to):
        return remote(gsum.at[to], grecv.at[s], gsend.at[to], grecv_sem.at[s], z, to)

    for k in range(1, S):
        grain_copy(lax.rem(s + k, S)).start()

    stage_c(1)
    if events >= 2:
        stage_b(2)
    if events >= 3:
        stage_a(3)
    best[...] = jnp.full_like(best, -1e30)
    score(z)

    for k in range(1, S):
        source = lax.rem(s + k, S)
        remote(
            gsum.at[source], grecv.at[source], gsend.at[source], grecv_sem.at[source], z, source
        ).wait_recv()
    grecv[s] = gsum[s]
    held = jnp.zeros((rows_out, pix), F32)
    for k in range(S):
        held = held + grecv[k].astype(F32)
    zbuf[z] = held.astype(BF16)

    def z_grain(to, at):
        return remote(zbuf.at[at], zbuf.at[at], zgsend.at[to], zgrecv.at[at], to, s)

    for k in range(1, D):
        z_grain(lax.rem(z + k, D), z).start()

    if events >= 2:
        stage_c(2)
    if events >= 3:
        stage_b(3)
    stage_d(1)
    if events >= 2:
        stage_d(2)

    for k in range(1, D):
        source = lax.rem(z + k, D)
        z_grain(source, source).wait_recv()
    held = jnp.zeros((rows_out, pix), F32)
    for k in range(D):
        held = held + zbuf[k].astype(F32)
    grain_out[...] = unit(held, pix)

    if events >= 3:
        stage_c(3)
        stage_d(3)
    if D > 4:
        @pl.loop(4, D)
        def _(e):
            stage_a(e)
            stage_b(e)
            stage_c(e)
            stage_d(e)

    score_row = best[...] * (1.0 / pix**0.5)
    for k in range(TR):
        score_out[k : k + 1, :] = score_row[:, k * TC : (k + 1) * TC]

    @pl.when(z < D - 1)
    def _():
        z_copy(z, z, z + 1).wait_send()

    @pl.when(z > 0)
    def _():
        z_copy(z, D, z - 1).wait_send()

    @pl.loop(1, D)
    def _(e):
        stage_end(e)

    for k in range(8):
        @pl.when(inside(halo_moves[k][2], halo_moves[k][3]))
        def _():
            halo_copy(k).wait_send()

    for k in range(1, S):
        grain_copy(lax.rem(s + k, S)).wait_send()
    for k in range(1, D):
        z_grain(lax.rem(z + k, D), z).wait_send()


def shards(D, S, patterns, background, templates, grain_id, keep_mask, grain_row):
    TR, TC, pix = patterns.shape
    R = templates.shape[0]
    G = grain_row.shape[0]
    rows_out = G // S
    points = TR * TC
    each = R // GROUP
    dma = pltpu.SemaphoreType.DMA
    vmem = pl.BlockSpec(memory_space=pltpu.VMEM)
    anywhere = pl.BlockSpec(memory_space=pl.ANY)
    return pl.pallas_call(
        functools.partial(kernel, D, S, G, TR, TC, pix, R),
        out_shape=(
            jax.ShapeDtypeStruct((TR, TC), F32),
            jax.ShapeDtypeStruct((rows_out, pix), F32),
        ),
        in_specs=[anywhere, anywhere, vmem, vmem, vmem, vmem],
        out_specs=(vmem, vmem),
        scratch_shapes=[
            pltpu.VMEM((TR, TC, pix), F32),
            pltpu.VMEM((GROUP, each, pix), BF16),
            pltpu.VMEM((TR, TC, pix), BF16),
            pltpu.VMEM((points, points), BF16),
            pltpu.VMEM((48, points), BF16),
            pltpu.VMEM((points, 128), BF16),
            pltpu.VMEM((G, points), BF16),
            pltpu.VMEM((2, 16, pix), BF16),
            pltpu.VMEM((4, 2, pix), BF16),
            pltpu.VMEM((4, 2, pix), BF16),
            pltpu.VMEM((8, 16, pix), BF16),
            pltpu.VMEM((points, pix), F32),
            pltpu.VMEM((points, pix), BF16),
            pltpu.VMEM((D, GROUP, each, pix), BF16),
            pltpu.VMEM((S, rows_out, pix), BF16),
            pltpu.VMEM((S, rows_out, pix), BF16),
            pltpu.VMEM((D, rows_out, pix), BF16),
            pltpu.VMEM((1, points), F32),
            dma((TR,)),
            dma,
            dma((D + 1,)),
            dma((D, 7)),
            dma((D, GROUP)),
            dma((8,)),
            dma((8,)),
            dma((S,)),
            dma((S,)),
            dma((D,)),
            dma((D,)),
        ],
        compiler_params=pltpu.CompilerParams(
            collective_id=0, has_side_effects=True, vmem_limit_bytes=56 * 1024 * 1024
        ),
    )(
        patterns,
        templates.reshape(GROUP, each, pix),
        background.reshape(1, pix),
        grain_id,
        keep_mask,
        grain_row.reshape(1, G),
    )


def solution(mesh):
    D, S = mesh.shape["dict"], mesh.shape["scan"]
    return jax.shard_map(
        functools.partial(shards, D, S),
        mesh=mesh,
        in_specs=(
            P("scan", "dict", None),
            P(),
            P("dict", None),
            P("scan", "dict"),
            P("scan", "dict"),
            P(),
        ),
        out_specs=(P("scan", "dict"), P("scan", None)),
        check_vma=False,
    )
```

```python
import functools

import jax
import jax.numpy as jnp
from jax import lax
from jax.experimental import pallas as pl
from jax.experimental.pallas import tpu as pltpu
from jax.sharding import PartitionSpec as P

MESH = pl.DeviceIdType.MESH
EPS = 1e-05
GROUP = 8
F32 = jnp.float32
BF16 = jnp.bfloat16


def iota(shape, dim):
    return lax.broadcasted_iota(jnp.int32, shape, dim)


def near(a, b):
    return (a - b <= 1) & (b - a <= 1)


def unit(values, pixels):
    square = jnp.sum(values * values, axis=-1, keepdims=True) * (1.0 / pixels)
    return values * lax.rsqrt(square + EPS)


def centred(values, pixels):
    return values - jnp.sum(values, axis=-1, keepdims=True) * (1.0 / pixels)


def kernel(
    D, S, G, TR, TC, pix, R,
    patterns, templates, background, grain_id, keep_mask, grain_row,
    score_out, grain_out,
    pat, raw, ground, filt, near_mat, pick_mat, halo_mat, sel_mat,
    edge, corner_src, corner_dst, halo, neigh, indexed, panel,
    gsum, grecv, zbuf, best,
    pat_sem, raw_sem, ground_sem, zsend, nsend, trecv, hsend, hrecv,
    gsend, grecv_sem, zgsend, zgrecv,
):
    z = lax.axis_index("dict")
    s = lax.axis_index("scan")
    points = TR * TC
    rows_out = G // S
    run = panel.shape[2]
    wide_pix = run * GROUP
    cuts = [(a, min(a + 512, pix)) for a in range(0, pix, 512)]

    def pat_copy(i):
        return pltpu.make_async_copy(patterns.at[i], pat.at[i], pat_sem.at[i])

    raw_copy = pltpu.make_async_copy(templates, raw, raw_sem)
    raw_copy.start()
    ground_copy = pltpu.make_async_copy(background, ground.at[0], ground_sem)
    ground_copy.start()
    for i in [TR - 1] + list(range(TR - 1)):
        pat_copy(i).start()

    halo[...] = jnp.zeros_like(halo)
    tail = pix // 128 * 128
    indexed[:, tail:] = jnp.zeros((points, wide_pix - tail), BF16)

    barrier = pltpu.get_barrier_semaphore()

    def hello(zz, ss):
        pl.semaphore_signal(
            barrier, inc=1, device_id={"dict": zz, "scan": ss}, device_id_type=MESH
        )

    for k in range(1, S):
        hello(z, lax.rem(s + k, S))
    for k in range(1, D):
        hello(lax.rem(z + k, D), s)
    diagonals = [(-1, -1), (-1, 1), (1, -1), (1, 1)]

    def inside(ds, dz):
        ok = None
        for cond in (
            [s >= 1] if ds < 0 else [s <= S - 2] if ds > 0 else []
        ) + ([z >= 1] if dz < 0 else [z <= D - 2] if dz > 0 else []):
            ok = cond if ok is None else ok & cond
        return ok

    for ds, dz in diagonals:
        @pl.when(inside(ds, dz))
        def _():
            hello(z + dz, s + ds)

    bits, low = TC.bit_length() - 1, TC - 1
    p0, q1 = iota((points, points), 0), iota((points, points), 1)
    near_mat[...] = jnp.where(
        near(p0 >> bits, q1 >> bits) & near(p0 & low, q1 & low), 1.0, 0.0
    ).astype(BF16)
    i0, q = iota((48, points), 0), iota((48, points), 1)
    k0 = (i0 - 32) >> 1
    corner_at = jnp.where(
        k0 == 0, 0, jnp.where(k0 == 1, TC - 1, jnp.where(k0 == 2, points - TC, points - 1))
    )
    want = jnp.where(
        i0 < 16, i0 * TC, jnp.where(i0 < 32, (i0 - 16) * TC + TC - 1,
                                    jnp.where(i0 < 40, corner_at, -1))
    )
    pick_mat[...] = jnp.where(q == want, 1.0, 0.0).astype(BF16)
    p, h = iota((points, 128), 0), iota((points, 128), 1)
    slot, i = h >> 4, h & 15
    r, c = p >> bits, p & low
    side = (
        ((slot == 0) & (r == 0) & near(c, i))
        | ((slot == 1) & (r == TR - 1) & near(c, i))
        | ((slot == 2) & (c == 0) & near(r, i))
        | ((slot == 3) & (c == TC - 1) & near(r, i))
        | ((slot == 4) & (i == 0) & (p == 0))
        | ((slot == 5) & (i == 0) & (p == TC - 1))
        | ((slot == 6) & (i == 0) & (p == points - TC))
        | ((slot == 7) & (i == 0) & (p == points - 1))
    )
    halo_mat[...] = jnp.where(side, 1.0, 0.0).astype(BF16)
    code = jnp.where(keep_mask[...] == 1, grain_id[...], -1).astype(F32).astype(BF16)
    spread = jnp.where((iota((TC, points), 1) & low) == iota((TC, points), 0), 1.0, 0.0).astype(BF16)
    wide = jnp.dot(code, spread, preferred_element_type=F32)
    own = (iota((TR, points), 1) >> bits) == iota((TR, points), 0)
    code_row = jnp.sum(jnp.where(own, wide, 0.0), axis=0, keepdims=True)
    one_hot = jnp.where(
        iota((G, points), 0).astype(F32) == code_row, 1.0, 0.0
    ).astype(BF16)
    to_row = jnp.where(iota((G, G), 0) == grain_row[...], 1.0, 0.0).astype(BF16)
    sel_mat[...] = jnp.dot(to_row, one_hot, preferred_element_type=F32).astype(BF16)

    piece = lax.rem(s, GROUP)
    base = s - piece
    core = lax.rem(piece, 2)
    xbit = lax.rem(piece // 2, 2)
    ybit = piece // 4
    px, py = piece + 2 - 4 * xbit, piece + 4 - 8 * ybit
    first = jnp.where(core == 0, px, py)
    second = jnp.where(core == 0, py, px)
    twin = 1 - 2 * core
    across = first + second - piece

    def remote(src, dst, ssem, rsem, zz, ss):
        return pltpu.make_async_remote_copy(
            src_ref=src, dst_ref=dst, send_sem=ssem, recv_sem=rsem,
            device_id={"dict": zz, "scan": ss}, device_id_type=MESH,
        )

    def shard_copy(d, q, ssem, zz, ss):
        return remote(panel.at[d, q], panel.at[d, q], ssem, trecv.at[d, q], zz, ss)

    def z_copy(d, sem_at, zz):
        return shard_copy(d, piece, zsend.at[sem_at], zz, s)

    def normalise():
        mean = jnp.sum(raw[...].astype(F32), axis=0, keepdims=True) * (1.0 / pix)
        off = raw[...].astype(F32) - mean
        square = jnp.sum(off * off, axis=0, keepdims=True) * (1.0 / pix)
        gain = lax.rsqrt(square + EPS)
        for j in range(GROUP):
            a, b = j * run, min((j + 1) * run, pix)
            panel[z, j, 0 : b - a, :] = ((raw[a:b, :].astype(F32) - mean) * gain).astype(BF16)
            if b - a < run:
                panel[z, j, b - a : run, :] = jnp.zeros((run - b + a, R), BF16)

    near_end = jnp.minimum(z, D - 1 - z)

    def event_shard(e):
        paired = e <= 2 * near_end
        k = jnp.where(paired, (e + 1) // 2, e - near_end)
        lower = jnp.where(paired, e % 2 == 1, z > near_end)
        return jnp.where(lower, z - k, z + k)

    def relay(d):
        target = jnp.where(d < z, z + 1, z - 1)
        return (target >= 0) & (target < D), target

    def piece_sends(d):
        return [
            (piece, 0, first), (piece, 1, second), (piece, 2, piece + twin),
            (first, 3, second), (first, 4, piece + twin),
            (second, 5, piece + twin), (across, 6, piece + twin),
        ]

    def in_plane(d, which):
        q, k, to = piece_sends(d)[which]
        return shard_copy(d, q, nsend.at[d, k], z, base + to)

    def arrived(d, q):
        shard_copy(d, q, nsend.at[d, 0], z, base + first).wait_recv()

    def stage_a(e):
        d = event_shard(e)
        arrived(d, piece)
        on, target = relay(d)

        @pl.when(on)
        def _():
            z_copy(d, d, target).start()

        for which in (0, 1, 2):
            in_plane(d, which).start()

    def stage_b(e):
        d = event_shard(e)
        arrived(d, first)
        for which in (3, 4):
            in_plane(d, which).start()

    def stage_c(e):
        d = event_shard(e)
        arrived(d, second)
        in_plane(d, 5).start()
        arrived(d, across)
        in_plane(d, 6).start()

    def score(d):
        dots = jnp.dot(
            indexed[...], panel[d].reshape(wide_pix, R), preferred_element_type=F32
        )
        best[...] = jnp.maximum(best[...], dots)

    def stage_d(e):
        d = event_shard(e)
        for q in (piece, first, second, across):
            arrived(d, q + twin)
        score(d)

    def stage_end(e):
        d = event_shard(e)
        on, target = relay(d)

        @pl.when(on)
        def _():
            z_copy(d, d, target).wait_send()

        for which in range(7):
            in_plane(d, which).wait_send()

    halo_moves = [
        (filt.at[TR - 1], halo.at[0], 1, 0),
        (filt.at[0], halo.at[1], -1, 0),
        (edge.at[1], halo.at[2], 0, 1),
        (edge.at[0], halo.at[3], 0, -1),
        (corner_src.at[3], corner_dst.at[0], 1, 1),
        (corner_src.at[2], corner_dst.at[1], 1, -1),
        (corner_src.at[1], corner_dst.at[2], -1, 1),
        (corner_src.at[0], corner_dst.at[3], -1, -1),
    ]

    def halo_copy(k):
        src, dst, ds, dz = halo_moves[k]
        return remote(src, dst, hsend.at[k], hrecv.at[k], z + dz, s + ds)

    def halo_send(k):
        @pl.when(inside(halo_moves[k][2], halo_moves[k][3]))
        def _():
            halo_copy(k).start()

    diag_count = sum(
        [jnp.where(inside(ds, dz), 1, 0) for ds, dz in diagonals]
    )
    raw_copy.wait()
    normalise()
    pl.semaphore_wait(barrier, S - 1 + D - 1 + diag_count)


    @pl.when(z < D - 1)
    def _():
        z_copy(z, z, z + 1).start()

    @pl.when(z > 0)
    def _():
        z_copy(z, D, z - 1).start()

    def filter_rows(a, b):
        for i in range(a, b):
            pat_copy(i).wait()
        centre = centred(pat[a:b] - ground[...].reshape(1, 1, pix), pix)
        filt[a:b] = unit(centre, pix).astype(BF16)

    ground_copy.wait()
    filter_rows(TR - 1, TR)
    halo_send(0)
    filter_rows(0, 1)
    halo_send(1)
    for a in range(1, TR - 1, 7):
        filter_rows(a, min(a + 7, TR - 1))

    for a, b in cuts:
        got = jnp.dot(
            pick_mat[...], filt[:, :, a:b].reshape(points, b - a), preferred_element_type=F32
        ).astype(BF16)
        edge[0, :, a:b] = got[0:16]
        edge[1, :, a:b] = got[16:32]
        for k in range(4):
            corner_src[k, :, a:b] = got[32 + 2 * k : 34 + 2 * k]
    for k in range(2, 8):
        halo_send(k)

    events = min(D - 1, 3)
    stage_a(1)

    for a, b in cuts:
        neigh[:, a:b] = jnp.dot(
            near_mat[...], filt[:, :, a:b].reshape(points, b - a), preferred_element_type=F32
        )
    stage_b(1)
    if events >= 2:
        stage_a(2)

    for k in range(8):
        ds, dz = halo_moves[k][2], halo_moves[k][3]

        @pl.when(inside(-ds, -dz))
        def _():
            halo_copy(k).wait_recv()
            if k >= 4:
                halo[k, 0:2, :] = corner_dst[k - 4]

    total = jnp.zeros((points, 1), F32)
    for a, b in cuts:
        part = neigh[:, a:b] + jnp.dot(
            halo_mat[...], halo[:, :, a:b].reshape(128, b - a), preferred_element_type=F32
        )
        neigh[:, a:b] = part
        total = total + jnp.sum(part * part, axis=1, keepdims=True)
    scale = lax.rsqrt(total * (1.0 / pix) + EPS)
    for a, b in cuts:
        indexed[:, a:b] = (neigh[:, a:b] * scale).astype(BF16)

    for a, b in cuts:
        sums = jnp.dot(sel_mat[...], indexed[:, a:b], preferred_element_type=F32).astype(BF16)
        for k in range(S):
            gsum[k, :, a:b] = sums[k * rows_out : (k + 1) * rows_out]

    def grain_copy(to):
        return remote(gsum.at[to], grecv.at[s], gsend.at[to], grecv_sem.at[s], z, to)

    for k in range(1, S):
        grain_copy(lax.rem(s + k, S)).start()

    stage_c(1)
    if events >= 2:
        stage_b(2)
    if events >= 3:
        stage_a(3)
    best[...] = jnp.full_like(best, -1e30)
    score(z)

    for k in range(1, S):
        source = lax.rem(s + k, S)
        remote(
            gsum.at[source], grecv.at[source], gsend.at[source], grecv_sem.at[source], z, source
        ).wait_recv()
    grecv[s] = gsum[s]
    held = jnp.zeros((rows_out, pix), F32)
    for k in range(S):
        held = held + grecv[k].astype(F32)
    zbuf[z] = held.astype(BF16)

    def z_grain(to, at):
        return remote(zbuf.at[at], zbuf.at[at], zgsend.at[to], zgrecv.at[at], to, s)

    for k in range(1, D):
        z_grain(lax.rem(z + k, D), z).start()

    if events >= 2:
        stage_c(2)
    if events >= 3:
        stage_b(3)
    stage_d(1)
    if events >= 2:
        stage_d(2)

    for k in range(1, D):
        source = lax.rem(z + k, D)
        z_grain(source, source).wait_recv()
    held = jnp.zeros((rows_out, pix), F32)
    for k in range(D):
        held = held + zbuf[k].astype(F32)
    grain_out[...] = unit(held, pix)

    if events >= 3:
        stage_c(3)
        stage_d(3)
    if D > 4:
        @pl.loop(4, D)
        def _(e):
            stage_a(e)
            stage_b(e)
            stage_c(e)
            stage_d(e)

    score_row = jnp.max(best[...].T, axis=0, keepdims=True) * (1.0 / pix**0.5)
    for k in range(TR):
        score_out[k : k + 1, :] = score_row[:, k * TC : (k + 1) * TC]

    @pl.when(z < D - 1)
    def _():
        z_copy(z, z, z + 1).wait_send()

    @pl.when(z > 0)
    def _():
        z_copy(z, D, z - 1).wait_send()

    @pl.loop(1, D)
    def _(e):
        stage_end(e)

    for k in range(8):
        @pl.when(inside(halo_moves[k][2], halo_moves[k][3]))
        def _():
            halo_copy(k).wait_send()

    for k in range(1, S):
        grain_copy(lax.rem(s + k, S)).wait_send()
    for k in range(1, D):
        z_grain(lax.rem(z + k, D), z).wait_send()


def hand_over(found, sums, score_out, grain_out):
    score_out[...] = found[...]
    grain_out[...] = sums[...]


def shards(D, S, patterns, background, templates, grain_id, keep_mask, grain_row):
    TR, TC, pix = patterns.shape
    R = templates.shape[0]
    G = grain_row.shape[0]
    rows_out = G // S
    points = TR * TC
    run = -(-pix // (GROUP * 16)) * 16
    dma = pltpu.SemaphoreType.DMA
    vmem = pl.BlockSpec(memory_space=pltpu.VMEM)
    anywhere = pl.BlockSpec(memory_space=pl.ANY)
    found, sums = pl.pallas_call(
        functools.partial(kernel, D, S, G, TR, TC, pix, R),
        out_shape=(
            jax.ShapeDtypeStruct((TR, TC), F32),
            jax.ShapeDtypeStruct((rows_out, pix), F32),
        ),
        in_specs=[anywhere, anywhere, anywhere, vmem, vmem, vmem],
        out_specs=(vmem, vmem),
        scratch_shapes=[
            pltpu.VMEM((TR, TC, pix), F32),
            pltpu.VMEM((pix, R), BF16),
            pltpu.VMEM((1, pix), F32),
            pltpu.VMEM((TR, TC, pix), BF16),
            pltpu.VMEM((points, points), BF16),
            pltpu.VMEM((48, points), BF16),
            pltpu.VMEM((points, 128), BF16),
            pltpu.VMEM((G, points), BF16),
            pltpu.VMEM((2, 16, pix), BF16),
            pltpu.VMEM((4, 2, pix), BF16),
            pltpu.VMEM((4, 2, pix), BF16),
            pltpu.VMEM((8, 16, pix), BF16),
            pltpu.VMEM((points, pix), F32),
            pltpu.VMEM((points, run * GROUP), BF16),
            pltpu.VMEM((D, GROUP, run, R), BF16),
            pltpu.VMEM((S, rows_out, pix), BF16),
            pltpu.VMEM((S, rows_out, pix), BF16),
            pltpu.VMEM((D, rows_out, pix), BF16),
            pltpu.VMEM((points, R), F32),
            dma((TR,)),
            dma,
            dma,
            dma((D + 1,)),
            dma((D, 7)),
            dma((D, GROUP)),
            dma((8,)),
            dma((8,)),
            dma((S,)),
            dma((S,)),
            dma((D,)),
            dma((D,)),
        ],
        compiler_params=pltpu.CompilerParams(
            collective_id=0, has_side_effects=True, vmem_limit_bytes=56 * 1024 * 1024
        ),
    )(
        patterns,
        templates.T,
        background,
        grain_id,
        keep_mask,
        grain_row.reshape(1, G),
    )
    return pl.pallas_call(
        hand_over,
        out_shape=(
            jax.ShapeDtypeStruct(found.shape, F32),
            jax.ShapeDtypeStruct(sums.shape, F32),
        ),
        in_specs=[vmem, vmem],
        out_specs=(vmem, vmem),
    )(found, sums)


def solution(mesh):
    D, S = mesh.shape["dict"], mesh.shape["scan"]
    return jax.shard_map(
        functools.partial(shards, D, S),
        mesh=mesh,
        in_specs=(
            P("scan", "dict", None),
            P(),
            P("dict", None),
            P("scan", "dict"),
            P("scan", "dict"),
            P(),
        ),
        out_specs=(P("scan", "dict"), P("scan", None)),
        check_vma=False,
    )
```

```python
import functools

import jax
import jax.numpy as jnp
from jax import lax
from jax.experimental import pallas as pl
from jax.experimental.pallas import tpu as pltpu
from jax.sharding import PartitionSpec as P

MESH = pl.DeviceIdType.MESH
EPS = 1e-05
GROUP = 8
F32 = jnp.float32
BF16 = jnp.bfloat16


def iota(shape, dim):
    return lax.broadcasted_iota(jnp.int32, shape, dim)


def near(a, b):
    return (a - b <= 1) & (b - a <= 1)


def unit(values, pixels):
    square = jnp.sum(values * values, axis=-1, keepdims=True) * (1.0 / pixels)
    return values * lax.rsqrt(square + EPS)


def centred(values, pixels):
    return values - jnp.sum(values, axis=-1, keepdims=True) * (1.0 / pixels)


def kernel(
    D, S, G, TR, TC, pix, R,
    patterns, templates, background, grain_id, keep_mask, grain_row,
    score_out, grain_out,
    pat, raw, ground, filt, near_mat, halo_mat, sel_mat,
    edge_rows, edge, corner_src, corner_dst, halo, neigh, indexed, panel,
    gsum, grecv, zbuf, best,
    pat_sem, raw_sem, ground_sem, zsend, nsend, trecv, hsend, hrecv,
    gsend, grecv_sem, zgsend, zgrecv,
):
    z = lax.axis_index("dict")
    s = lax.axis_index("scan")
    points = TR * TC
    rows_out = G // S
    run = panel.shape[2]
    wide_pix = run * GROUP
    cuts = [(a, min(a + 512, pix)) for a in range(0, pix, 512)]

    def pat_copy(i):
        return pltpu.make_async_copy(patterns.at[i], pat.at[i], pat_sem.at[i])

    raw_copy = pltpu.make_async_copy(templates, raw, raw_sem)
    raw_copy.start()
    ground_copy = pltpu.make_async_copy(background, ground.at[0], ground_sem)
    ground_copy.start()
    for i in [TR - 1] + list(range(TR - 1)):
        pat_copy(i).start()

    halo[...] = jnp.zeros_like(halo)
    tail = pix // 128 * 128
    indexed[:, tail:] = jnp.zeros((points, wide_pix - tail), BF16)

    barrier = pltpu.get_barrier_semaphore()

    def hello(zz, ss):
        pl.semaphore_signal(
            barrier, inc=1, device_id={"dict": zz, "scan": ss}, device_id_type=MESH
        )

    for k in range(1, S):
        hello(z, lax.rem(s + k, S))
    for k in range(1, D):
        hello(lax.rem(z + k, D), s)
    diagonals = [(-1, -1), (-1, 1), (1, -1), (1, 1)]

    def inside(ds, dz):
        ok = None
        for cond in (
            [s >= 1] if ds < 0 else [s <= S - 2] if ds > 0 else []
        ) + ([z >= 1] if dz < 0 else [z <= D - 2] if dz > 0 else []):
            ok = cond if ok is None else ok & cond
        return ok

    for ds, dz in diagonals:
        @pl.when(inside(ds, dz))
        def _():
            hello(z + dz, s + ds)

    bits, low = TC.bit_length() - 1, TC - 1
    p0, q1 = iota((points, points), 0), iota((points, points), 1)
    near_mat[...] = jnp.where(
        near(p0 >> bits, q1 >> bits) & near(p0 & low, q1 & low), 1.0, 0.0
    ).astype(BF16)
    p, h = iota((points, 128), 0), iota((points, 128), 1)
    slot, i = h >> 4, h & 15
    r, c = p >> bits, p & low
    side = (
        ((slot == 0) & (r == 0) & near(c, i))
        | ((slot == 1) & (r == TR - 1) & near(c, i))
        | ((slot == 2) & (c == 0) & near(r, i))
        | ((slot == 3) & (c == TC - 1) & near(r, i))
        | ((slot == 4) & (i == 0) & (p == 0))
        | ((slot == 5) & (i == 0) & (p == TC - 1))
        | ((slot == 6) & (i == 0) & (p == points - TC))
        | ((slot == 7) & (i == 0) & (p == points - 1))
    )
    halo_mat[...] = jnp.where(side, 1.0, 0.0).astype(BF16)
    code = jnp.where(keep_mask[...] == 1, grain_id[...], -1).astype(F32).astype(BF16)
    spread = jnp.where((iota((TC, points), 1) & low) == iota((TC, points), 0), 1.0, 0.0).astype(BF16)
    wide = jnp.dot(code, spread, preferred_element_type=F32)
    own = (iota((TR, points), 1) >> bits) == iota((TR, points), 0)
    code_row = jnp.sum(jnp.where(own, wide, 0.0), axis=0, keepdims=True)
    one_hot = jnp.where(
        iota((G, points), 0).astype(F32) == code_row, 1.0, 0.0
    ).astype(BF16)
    to_row = jnp.where(iota((G, G), 0) == grain_row[...], 1.0, 0.0).astype(BF16)
    sel_mat[...] = jnp.dot(to_row, one_hot, preferred_element_type=F32).astype(BF16)

    piece = lax.rem(s, GROUP)
    base = s - piece
    core = lax.rem(piece, 2)
    xbit = lax.rem(piece // 2, 2)
    ybit = piece // 4
    px, py = piece + 2 - 4 * xbit, piece + 4 - 8 * ybit
    first = jnp.where(core == 0, px, py)
    second = jnp.where(core == 0, py, px)
    twin = 1 - 2 * core
    across = first + second - piece

    def remote(src, dst, ssem, rsem, zz, ss):
        return pltpu.make_async_remote_copy(
            src_ref=src, dst_ref=dst, send_sem=ssem, recv_sem=rsem,
            device_id={"dict": zz, "scan": ss}, device_id_type=MESH,
        )

    def shard_copy(d, q, ssem, zz, ss):
        return remote(panel.at[d, q], panel.at[d, q], ssem, trecv.at[d, q], zz, ss)

    def z_copy(zz):
        return shard_copy(z, piece, zsend.at[zz], zz, s)

    def z_each(k, act):
        for step in (k, -k):
            @pl.when((z + step >= 0) & (z + step < D))
            def _():
                act(z_copy(z + step))

    def normalise():
        mean = jnp.sum(raw[...].astype(F32), axis=0, keepdims=True) * (1.0 / pix)
        off = raw[...].astype(F32) - mean
        square = jnp.sum(off * off, axis=0, keepdims=True) * (1.0 / pix)
        gain = lax.rsqrt(square + EPS)
        for j in range(GROUP):
            a, b = j * run, min((j + 1) * run, pix)
            panel[z, j, 0 : b - a, :] = ((raw[a:b, :].astype(F32) - mean) * gain).astype(BF16)
            if b - a < run:
                panel[z, j, b - a : run, :] = jnp.zeros((run - b + a, R), BF16)

    near_end = jnp.minimum(z, D - 1 - z)

    def event_shard(e):
        paired = e <= 2 * near_end
        k = jnp.where(paired, (e + 1) // 2, e - near_end)
        lower = jnp.where(paired, e % 2 == 1, z > near_end)
        return jnp.where(lower, z - k, z + k)

    def piece_sends(d):
        return [
            (piece, 0, first), (piece, 1, second), (piece, 2, piece + twin),
            (first, 3, second), (first, 4, piece + twin),
            (second, 5, piece + twin), (across, 6, piece + twin),
        ]

    def in_plane(d, which):
        q, k, to = piece_sends(d)[which]
        return shard_copy(d, q, nsend.at[d, k], z, base + to)

    def arrived(d, q):
        shard_copy(d, q, nsend.at[d, 0], z, base + first).wait_recv()

    def stage_a(e):
        d = event_shard(e)
        arrived(d, piece)
        for which in (0, 1, 2):
            in_plane(d, which).start()

    def stage_b(e):
        d = event_shard(e)
        arrived(d, first)
        for which in (3, 4):
            in_plane(d, which).start()

    def stage_c(e):
        d = event_shard(e)
        arrived(d, second)
        in_plane(d, 5).start()
        arrived(d, across)
        in_plane(d, 6).start()

    def score(d):
        dots = jnp.dot(
            indexed[...], panel[d].reshape(wide_pix, R), preferred_element_type=F32
        )
        best[...] = jnp.maximum(best[...], dots)

    def stage_d(e):
        d = event_shard(e)
        for q in (piece, first, second, across):
            arrived(d, q + twin)
        score(d)

    def stage_end(e):
        d = event_shard(e)
        for which in range(7):
            in_plane(d, which).wait_send()

    halo_moves = [
        (filt.at[TR - 1], halo.at[0], 1, 0),
        (filt.at[0], halo.at[1], -1, 0),
        (edge.at[1], halo.at[2], 0, 1),
        (edge.at[0], halo.at[3], 0, -1),
        (corner_src.at[3], corner_dst.at[0], 1, 1),
        (corner_src.at[2], corner_dst.at[1], 1, -1),
        (corner_src.at[1], corner_dst.at[2], -1, 1),
        (corner_src.at[0], corner_dst.at[3], -1, -1),
    ]

    def halo_copy(k):
        src, dst, ds, dz = halo_moves[k]
        return remote(src, dst, hsend.at[k], hrecv.at[k], z + dz, s + ds)

    def halo_send(k):
        @pl.when(inside(halo_moves[k][2], halo_moves[k][3]))
        def _():
            halo_copy(k).start()

    diag_count = sum(
        [jnp.where(inside(ds, dz), 1, 0) for ds, dz in diagonals]
    )
    raw_copy.wait()
    normalise()
    pl.semaphore_wait(barrier, S - 1 + D - 1 + diag_count)


    z_each(1, lambda copy: copy.start())

    def filter_rows(a, b):
        for i in range(a, b):
            pat_copy(i).wait()
        centre = centred(pat[a:b] - ground[...].reshape(1, 1, pix), pix)
        values = unit(centre, pix)
        filt[a:b] = values.astype(BF16)
        for i in range(a, b):
            edge_rows[0, i : i + 1, :] = values[i - a, 0:1, :]
            edge_rows[1, i : i + 1, :] = values[i - a, TC - 1 : TC, :]

    ground_copy.wait()
    filter_rows(TR - 1, TR)
    filter_rows(0, 1)
    halo_send(0)
    halo_send(1)
    for a in range(1, TR - 1, 7):
        filter_rows(a, min(a + 7, TR - 1))
    edge[...] = edge_rows[...].astype(BF16)
    for k, (side, i) in enumerate([(0, 0), (1, 0), (0, TR - 1), (1, TR - 1)]):
        corner_src[k] = jnp.broadcast_to(edge_rows[side, i : i + 1, :], (2, pix)).astype(BF16)
    for k in range(2, 8):
        halo_send(k)
    for k in range(2, D):
        z_each(k, lambda copy: copy.start())

    events = min(D - 1, 3)
    stage_a(1)

    for a, b in cuts:
        neigh[:, a:b] = jnp.dot(
            near_mat[...], filt[:, :, a:b].reshape(points, b - a), preferred_element_type=F32
        )
    stage_b(1)
    if events >= 2:
        stage_a(2)

    for k in range(8):
        ds, dz = halo_moves[k][2], halo_moves[k][3]

        @pl.when(inside(-ds, -dz))
        def _():
            halo_copy(k).wait_recv()
            if k >= 4:
                halo[k, 0:2, :] = corner_dst[k - 4]

    total = jnp.zeros((points, 1), F32)
    for a, b in cuts:
        part = neigh[:, a:b] + jnp.dot(
            halo_mat[...], halo[:, :, a:b].reshape(128, b - a), preferred_element_type=F32
        )
        neigh[:, a:b] = part
        total = total + jnp.sum(part * part, axis=1, keepdims=True)
    scale = lax.rsqrt(total * (1.0 / pix) + EPS)
    for a, b in cuts:
        indexed[:, a:b] = (neigh[:, a:b] * scale).astype(BF16)

    for a, b in cuts:
        sums = jnp.dot(sel_mat[...], indexed[:, a:b], preferred_element_type=F32).astype(BF16)
        for k in range(S):
            gsum[k, :, a:b] = sums[k * rows_out : (k + 1) * rows_out]

    def grain_copy(to):
        return remote(gsum.at[to], grecv.at[s], gsend.at[to], grecv_sem.at[s], z, to)

    for k in range(1, S):
        grain_copy(lax.rem(s + k, S)).start()

    stage_c(1)
    if events >= 2:
        stage_b(2)
    if events >= 3:
        stage_a(3)
    best[...] = jnp.full_like(best, -1e30)
    score(z)

    for k in range(1, S):
        source = lax.rem(s + k, S)
        remote(
            gsum.at[source], grecv.at[source], gsend.at[source], grecv_sem.at[source], z, source
        ).wait_recv()
    grecv[s] = gsum[s]
    held = jnp.zeros((rows_out, pix), F32)
    for k in range(S):
        held = held + grecv[k].astype(F32)
    zbuf[z] = held.astype(BF16)

    def z_grain(to, at):
        return remote(zbuf.at[at], zbuf.at[at], zgsend.at[to], zgrecv.at[at], to, s)

    for k in range(1, D):
        z_grain(lax.rem(z + k, D), z).start()

    if events >= 2:
        stage_c(2)
    if events >= 3:
        stage_b(3)
    stage_d(1)
    if events >= 2:
        stage_d(2)

    for k in range(1, D):
        source = lax.rem(z + k, D)
        z_grain(source, source).wait_recv()
    held = jnp.zeros((rows_out, pix), F32)
    for k in range(D):
        held = held + zbuf[k].astype(F32)
    grain_out[...] = unit(held, pix)

    if events >= 3:
        stage_c(3)
        stage_d(3)
    if D > 4:
        @pl.loop(4, D)
        def _(e):
            stage_a(e)
            stage_b(e)
            stage_c(e)
            stage_d(e)

    score_row = jnp.max(best[...].T, axis=0, keepdims=True) * (1.0 / pix**0.5)
    for k in range(TR):
        score_out[k : k + 1, :] = score_row[:, k * TC : (k + 1) * TC]

    for k in range(1, D):
        z_each(k, lambda copy: copy.wait_send())

    @pl.loop(1, D)
    def _(e):
        stage_end(e)

    for k in range(8):
        @pl.when(inside(halo_moves[k][2], halo_moves[k][3]))
        def _():
            halo_copy(k).wait_send()

    for k in range(1, S):
        grain_copy(lax.rem(s + k, S)).wait_send()
    for k in range(1, D):
        z_grain(lax.rem(z + k, D), z).wait_send()


def hand_over(found, sums, score_out, grain_out):
    score_out[...] = found[...]
    grain_out[...] = sums[...]


def shards(D, S, patterns, background, templates, grain_id, keep_mask, grain_row):
    TR, TC, pix = patterns.shape
    R = templates.shape[0]
    G = grain_row.shape[0]
    rows_out = G // S
    points = TR * TC
    run = -(-pix // (GROUP * 16)) * 16
    dma = pltpu.SemaphoreType.DMA
    vmem = pl.BlockSpec(memory_space=pltpu.VMEM)
    anywhere = pl.BlockSpec(memory_space=pl.ANY)
    found, sums = pl.pallas_call(
        functools.partial(kernel, D, S, G, TR, TC, pix, R),
        out_shape=(
            jax.ShapeDtypeStruct((TR, TC), F32),
            jax.ShapeDtypeStruct((rows_out, pix), F32),
        ),
        in_specs=[anywhere, anywhere, anywhere, vmem, vmem, vmem],
        out_specs=(vmem, vmem),
        scratch_shapes=[
            pltpu.VMEM((TR, TC, pix), F32),
            pltpu.VMEM((pix, R), BF16),
            pltpu.VMEM((1, pix), F32),
            pltpu.VMEM((TR, TC, pix), BF16),
            pltpu.VMEM((points, points), BF16),
            pltpu.VMEM((points, 128), BF16),
            pltpu.VMEM((G, points), BF16),
            pltpu.VMEM((2, 16, pix), F32),
            pltpu.VMEM((2, 16, pix), BF16),
            pltpu.VMEM((4, 2, pix), BF16),
            pltpu.VMEM((4, 2, pix), BF16),
            pltpu.VMEM((8, 16, pix), BF16),
            pltpu.VMEM((points, pix), F32),
            pltpu.VMEM((points, run * GROUP), BF16),
            pltpu.VMEM((D, GROUP, run, R), BF16),
            pltpu.VMEM((S, rows_out, pix), BF16),
            pltpu.VMEM((S, rows_out, pix), BF16),
            pltpu.VMEM((D, rows_out, pix), BF16),
            pltpu.VMEM((points, R), F32),
            dma((TR,)),
            dma,
            dma,
            dma((D,)),
            dma((D, 7)),
            dma((D, GROUP)),
            dma((8,)),
            dma((8,)),
            dma((S,)),
            dma((S,)),
            dma((D,)),
            dma((D,)),
        ],
        compiler_params=pltpu.CompilerParams(
            collective_id=0, has_side_effects=True, vmem_limit_bytes=56 * 1024 * 1024
        ),
    )(
        patterns,
        templates.T,
        background,
        grain_id,
        keep_mask,
        grain_row.reshape(1, G),
    )
    return pl.pallas_call(
        hand_over,
        out_shape=(
            jax.ShapeDtypeStruct(found.shape, F32),
            jax.ShapeDtypeStruct(sums.shape, F32),
        ),
        in_specs=[vmem, vmem],
        out_specs=(vmem, vmem),
    )(found, sums)


def solution(mesh):
    D, S = mesh.shape["dict"], mesh.shape["scan"]
    return jax.shard_map(
        functools.partial(shards, D, S),
        mesh=mesh,
        in_specs=(
            P("scan", "dict", None),
            P(),
            P("dict", None),
            P("scan", "dict"),
            P("scan", "dict"),
            P(),
        ),
        out_specs=(P("scan", "dict"), P("scan", None)),
        check_vma=False,
    )
```

```python
import functools

import jax
import jax.numpy as jnp
from jax import lax
from jax.experimental import pallas as pl
from jax.experimental.pallas import tpu as pltpu
from jax.sharding import PartitionSpec as P

MESH = pl.DeviceIdType.MESH
EPS = 1e-05
GROUP = 8
F32 = jnp.float32
BF16 = jnp.bfloat16


def iota(shape, dim):
    return lax.broadcasted_iota(jnp.int32, shape, dim)


def near(a, b):
    return (a - b <= 1) & (b - a <= 1)


def unit(values, pixels):
    square = jnp.sum(values * values, axis=-1, keepdims=True) * (1.0 / pixels)
    return values * lax.rsqrt(square + EPS)


def centred(values, pixels):
    return values - jnp.sum(values, axis=-1, keepdims=True) * (1.0 / pixels)


def kernel(
    D, S, G, TR, TC, pix, R,
    patterns, templates, background, grain_id, keep_mask, grain_row,
    score_out, grain_out,
    pat, raw, ground, filt, near_mat, halo_mat, sel_mat,
    edge_rows, edge, corner_src, corner_dst, halo, neigh, indexed, panel,
    gsum, grecv, zbuf, best,
    pat_sem, raw_sem, ground_sem, zsend, nsend, trecv, hsend, hrecv,
    gsend, grecv_sem, zgsend, zgrecv,
):
    z = lax.axis_index("dict")
    s = lax.axis_index("scan")
    points = TR * TC
    rows_out = G // S
    run = panel.shape[2]
    wide_pix = run * GROUP
    cuts = [(a, min(a + 512, pix)) for a in range(0, pix, 512)]

    def pat_copy(i):
        return pltpu.make_async_copy(patterns.at[i], pat.at[i], pat_sem.at[i])

    raw_copy = pltpu.make_async_copy(templates, raw, raw_sem)
    raw_copy.start()
    ground_copy = pltpu.make_async_copy(background, ground.at[0], ground_sem)
    ground_copy.start()
    for i in [TR - 1] + list(range(TR - 1)):
        pat_copy(i).start()

    halo[...] = jnp.zeros_like(halo)
    tail = pix // 128 * 128
    indexed[:, tail:] = jnp.zeros((points, wide_pix - tail), BF16)

    barrier = pltpu.get_barrier_semaphore()

    def hello(zz, ss):
        pl.semaphore_signal(
            barrier, inc=1, device_id={"dict": zz, "scan": ss}, device_id_type=MESH
        )

    for k in range(1, S):
        hello(z, lax.rem(s + k, S))
    for k in range(1, D):
        hello(lax.rem(z + k, D), s)
    diagonals = [(-1, -1), (-1, 1), (1, -1), (1, 1)]

    def inside(ds, dz):
        ok = None
        for cond in (
            [s >= 1] if ds < 0 else [s <= S - 2] if ds > 0 else []
        ) + ([z >= 1] if dz < 0 else [z <= D - 2] if dz > 0 else []):
            ok = cond if ok is None else ok & cond
        return ok

    for ds, dz in diagonals:
        @pl.when(inside(ds, dz))
        def _():
            hello(z + dz, s + ds)

    bits, low = TC.bit_length() - 1, TC - 1
    p0, q1 = iota((points, points), 0), iota((points, points), 1)
    near_mat[...] = jnp.where(
        near(p0 >> bits, q1 >> bits) & near(p0 & low, q1 & low), 1.0, 0.0
    ).astype(BF16)
    p, h = iota((points, 128), 0), iota((points, 128), 1)
    slot, i = h >> 4, h & 15
    r, c = p >> bits, p & low
    side = (
        ((slot == 0) & (r == 0) & near(c, i))
        | ((slot == 1) & (r == TR - 1) & near(c, i))
        | ((slot == 2) & (c == 0) & near(r, i))
        | ((slot == 3) & (c == TC - 1) & near(r, i))
        | ((slot == 4) & (i == 0) & (p == 0))
        | ((slot == 5) & (i == 0) & (p == TC - 1))
        | ((slot == 6) & (i == 0) & (p == points - TC))
        | ((slot == 7) & (i == 0) & (p == points - 1))
    )
    halo_mat[...] = jnp.where(side, 1.0, 0.0).astype(BF16)
    code = jnp.where(keep_mask[...] == 1, grain_id[...], -1).astype(F32).astype(BF16)
    spread = jnp.where((iota((TC, points), 1) & low) == iota((TC, points), 0), 1.0, 0.0).astype(BF16)
    wide = jnp.dot(code, spread, preferred_element_type=F32)
    own = (iota((TR, points), 1) >> bits) == iota((TR, points), 0)
    code_row = jnp.sum(jnp.where(own, wide, 0.0), axis=0, keepdims=True)
    one_hot = jnp.where(
        iota((G, points), 0).astype(F32) == code_row, 1.0, 0.0
    ).astype(BF16)
    to_row = jnp.where(iota((G, G), 0) == grain_row[...], 1.0, 0.0).astype(BF16)
    sel_mat[...] = jnp.dot(to_row, one_hot, preferred_element_type=F32).astype(BF16)

    piece = lax.rem(s, GROUP)
    base = s - piece
    core = lax.rem(piece, 2)
    xbit = lax.rem(piece // 2, 2)
    ybit = piece // 4
    px, py = piece + 2 - 4 * xbit, piece + 4 - 8 * ybit
    first = jnp.where(core == 0, px, py)
    second = jnp.where(core == 0, py, px)
    twin = 1 - 2 * core
    across = first + second - piece

    def remote(src, dst, ssem, rsem, zz, ss):
        return pltpu.make_async_remote_copy(
            src_ref=src, dst_ref=dst, send_sem=ssem, recv_sem=rsem,
            device_id={"dict": zz, "scan": ss}, device_id_type=MESH,
        )

    def shard_copy(d, q, ssem, zz, ss):
        return remote(panel.at[d, q], panel.at[d, q], ssem, trecv.at[d, q], zz, ss)

    def z_copy(zz):
        return shard_copy(z, piece, zsend.at[zz], zz, s)

    def z_each(k, act):
        for step in (k, -k):
            @pl.when((z + step >= 0) & (z + step < D))
            def _():
                act(z_copy(z + step))

    def normalise():
        mean = jnp.sum(raw[...].astype(F32), axis=0, keepdims=True) * (1.0 / pix)
        off = raw[...].astype(F32) - mean
        square = jnp.sum(off * off, axis=0, keepdims=True) * (1.0 / pix)
        gain = lax.rsqrt(square + EPS)
        for j in range(GROUP):
            a, b = j * run, min((j + 1) * run, pix)
            panel[z, j, 0 : b - a, :] = ((raw[a:b, :].astype(F32) - mean) * gain).astype(BF16)
            if b - a < run:
                panel[z, j, b - a : run, :] = jnp.zeros((run - b + a, R), BF16)

    near_end = jnp.minimum(z, D - 1 - z)

    def event_shard(e):
        paired = e <= 2 * near_end
        k = jnp.where(paired, (e + 1) // 2, e - near_end)
        lower = jnp.where(paired, e % 2 == 1, z > near_end)
        return jnp.where(lower, z - k, z + k)

    def piece_sends(d):
        return [
            (piece, 0, first), (piece, 1, second), (piece, 2, piece + twin),
            (piece, 3, across), (first, 4, piece + twin),
            (second, 5, piece + twin), (across, 6, piece + twin),
        ]

    def in_plane(d, which):
        q, k, to = piece_sends(d)[which]
        return shard_copy(d, q, nsend.at[d, k], z, base + to)

    def arrived(d, q):
        shard_copy(d, q, nsend.at[d, 0], z, base + first).wait_recv()

    def stage_a(e):
        d = event_shard(e)
        arrived(d, piece)
        for which in (0, 1, 3, 2):
            in_plane(d, which).start()

    def stage_b(e):
        d = event_shard(e)
        for q, which in ((first, 4), (second, 5), (across, 6)):
            arrived(d, q)
            in_plane(d, which).start()

    def score(d):
        dots = jnp.dot(
            indexed[...], panel[d].reshape(wide_pix, R), preferred_element_type=F32
        )
        best[...] = jnp.maximum(best[...], dots)

    def stage_d(e):
        d = event_shard(e)
        for q in (piece, first, second, across):
            arrived(d, q + twin)
        score(d)

    def stage_end(e):
        d = event_shard(e)
        for which in range(7):
            in_plane(d, which).wait_send()

    halo_moves = [
        (filt.at[TR - 1], halo.at[0], 1, 0),
        (filt.at[0], halo.at[1], -1, 0),
        (edge.at[1], halo.at[2], 0, 1),
        (edge.at[0], halo.at[3], 0, -1),
        (corner_src.at[3], corner_dst.at[0], 1, 1),
        (corner_src.at[2], corner_dst.at[1], 1, -1),
        (corner_src.at[1], corner_dst.at[2], -1, 1),
        (corner_src.at[0], corner_dst.at[3], -1, -1),
    ]

    def halo_copy(k):
        src, dst, ds, dz = halo_moves[k]
        return remote(src, dst, hsend.at[k], hrecv.at[k], z + dz, s + ds)

    def halo_send(k):
        @pl.when(inside(halo_moves[k][2], halo_moves[k][3]))
        def _():
            halo_copy(k).start()

    diag_count = sum(
        [jnp.where(inside(ds, dz), 1, 0) for ds, dz in diagonals]
    )
    raw_copy.wait()
    normalise()
    pl.semaphore_wait(barrier, S - 1 + D - 1 + diag_count)


    for k in range(1, min(D, 3)):
        z_each(k, lambda copy: copy.start())

    def filter_rows(a, b):
        for i in range(a, b):
            pat_copy(i).wait()
        centre = centred(pat[a:b] - ground[...].reshape(1, 1, pix), pix)
        values = unit(centre, pix)
        filt[a:b] = values.astype(BF16)
        for i in range(a, b):
            edge_rows[0, i : i + 1, :] = values[i - a, 0:1, :]
            edge_rows[1, i : i + 1, :] = values[i - a, TC - 1 : TC, :]

    ground_copy.wait()
    filter_rows(TR - 1, TR)
    filter_rows(0, 1)
    halo_send(0)
    halo_send(1)
    for a in range(1, TR - 1, 7):
        filter_rows(a, min(a + 7, TR - 1))
    edge[...] = edge_rows[...].astype(BF16)
    for k, (side, i) in enumerate([(0, 0), (1, 0), (0, TR - 1), (1, TR - 1)]):
        corner_src[k] = jnp.broadcast_to(edge_rows[side, i : i + 1, :], (2, pix)).astype(BF16)
    for k in range(2, 8):
        halo_send(k)
    for k in range(3, D):
        z_each(k, lambda copy: copy.start())

    events = min(D - 1, 3)
    stage_a(1)

    for a, b in cuts:
        neigh[:, a:b] = jnp.dot(
            near_mat[...], filt[:, :, a:b].reshape(points, b - a), preferred_element_type=F32
        )
    stage_b(1)
    if events >= 2:
        stage_a(2)

    for k in range(8):
        ds, dz = halo_moves[k][2], halo_moves[k][3]

        @pl.when(inside(-ds, -dz))
        def _():
            halo_copy(k).wait_recv()
            if k >= 4:
                halo[k, 0:2, :] = corner_dst[k - 4]

    total = jnp.zeros((points, 1), F32)
    for a, b in cuts:
        part = neigh[:, a:b] + jnp.dot(
            halo_mat[...], halo[:, :, a:b].reshape(128, b - a), preferred_element_type=F32
        )
        neigh[:, a:b] = part
        total = total + jnp.sum(part * part, axis=1, keepdims=True)
    scale = lax.rsqrt(total * (1.0 / pix) + EPS)
    for a, b in cuts:
        indexed[:, a:b] = (neigh[:, a:b] * scale).astype(BF16)

    for a, b in cuts:
        sums = jnp.dot(sel_mat[...], indexed[:, a:b], preferred_element_type=F32).astype(BF16)
        for k in range(S):
            gsum[k, :, a:b] = sums[k * rows_out : (k + 1) * rows_out]

    def grain_copy(to):
        return remote(gsum.at[to], grecv.at[s], gsend.at[to], grecv_sem.at[s], z, to)

    for k in range(1, S):
        grain_copy(lax.rem(s + k, S)).start()

    if events >= 2:
        stage_b(2)
    if events >= 3:
        stage_a(3)
    best[...] = jnp.full_like(best, -1e30)
    score(z)

    for k in range(1, S):
        source = lax.rem(s + k, S)
        remote(
            gsum.at[source], grecv.at[source], gsend.at[source], grecv_sem.at[source], z, source
        ).wait_recv()
    grecv[s] = gsum[s]
    held = jnp.zeros((rows_out, pix), F32)
    for k in range(S):
        held = held + grecv[k].astype(F32)
    zbuf[z] = held.astype(BF16)

    def z_grain(to, at):
        return remote(zbuf.at[at], zbuf.at[at], zgsend.at[to], zgrecv.at[at], to, s)

    for k in range(1, D):
        z_grain(lax.rem(z + k, D), z).start()

    stage_d(1)
    if events >= 3:
        stage_b(3)
    if events >= 2:
        stage_d(2)

    for k in range(1, D):
        source = lax.rem(z + k, D)
        z_grain(source, source).wait_recv()
    held = jnp.zeros((rows_out, pix), F32)
    for k in range(D):
        held = held + zbuf[k].astype(F32)
    grain_out[...] = unit(held, pix)

    if events >= 3:
        stage_d(3)
    if D > 4:
        @pl.loop(4, D)
        def _(e):
            stage_a(e)
            stage_b(e)
            stage_d(e)

    score_row = jnp.max(best[...].T, axis=0, keepdims=True) * (1.0 / pix**0.5)
    for k in range(TR):
        score_out[k : k + 1, :] = score_row[:, k * TC : (k + 1) * TC]

    for k in range(1, D):
        z_each(k, lambda copy: copy.wait_send())

    @pl.loop(1, D)
    def _(e):
        stage_end(e)

    for k in range(8):
        @pl.when(inside(halo_moves[k][2], halo_moves[k][3]))
        def _():
            halo_copy(k).wait_send()

    for k in range(1, S):
        grain_copy(lax.rem(s + k, S)).wait_send()
    for k in range(1, D):
        z_grain(lax.rem(z + k, D), z).wait_send()


def hand_over(found, sums, score_out, grain_out):
    score_out[...] = found[...]
    grain_out[...] = sums[...]


def shards(D, S, patterns, background, templates, grain_id, keep_mask, grain_row):
    TR, TC, pix = patterns.shape
    R = templates.shape[0]
    G = grain_row.shape[0]
    rows_out = G // S
    points = TR * TC
    run = -(-pix // (GROUP * 16)) * 16
    dma = pltpu.SemaphoreType.DMA
    vmem = pl.BlockSpec(memory_space=pltpu.VMEM)
    anywhere = pl.BlockSpec(memory_space=pl.ANY)
    found, sums = pl.pallas_call(
        functools.partial(kernel, D, S, G, TR, TC, pix, R),
        out_shape=(
            jax.ShapeDtypeStruct((TR, TC), F32),
            jax.ShapeDtypeStruct((rows_out, pix), F32),
        ),
        in_specs=[anywhere, anywhere, anywhere, vmem, vmem, vmem],
        out_specs=(vmem, vmem),
        scratch_shapes=[
            pltpu.VMEM((TR, TC, pix), F32),
            pltpu.VMEM((pix, R), BF16),
            pltpu.VMEM((1, pix), F32),
            pltpu.VMEM((TR, TC, pix), BF16),
            pltpu.VMEM((points, points), BF16),
            pltpu.VMEM((points, 128), BF16),
            pltpu.VMEM((G, points), BF16),
            pltpu.VMEM((2, 16, pix), F32),
            pltpu.VMEM((2, 16, pix), BF16),
            pltpu.VMEM((4, 2, pix), BF16),
            pltpu.VMEM((4, 2, pix), BF16),
            pltpu.VMEM((8, 16, pix), BF16),
            pltpu.VMEM((points, pix), F32),
            pltpu.VMEM((points, run * GROUP), BF16),
            pltpu.VMEM((D, GROUP, run, R), BF16),
            pltpu.VMEM((S, rows_out, pix), BF16),
            pltpu.VMEM((S, rows_out, pix), BF16),
            pltpu.VMEM((D, rows_out, pix), BF16),
            pltpu.VMEM((points, R), F32),
            dma((TR,)),
            dma,
            dma,
            dma((D,)),
            dma((D, 7)),
            dma((D, GROUP)),
            dma((8,)),
            dma((8,)),
            dma((S,)),
            dma((S,)),
            dma((D,)),
            dma((D,)),
        ],
        compiler_params=pltpu.CompilerParams(
            collective_id=0, has_side_effects=True, vmem_limit_bytes=56 * 1024 * 1024
        ),
    )(
        patterns,
        templates.T,
        background,
        grain_id,
        keep_mask,
        grain_row.reshape(1, G),
    )
    return pl.pallas_call(
        hand_over,
        out_shape=(
            jax.ShapeDtypeStruct(found.shape, F32),
            jax.ShapeDtypeStruct(sums.shape, F32),
        ),
        in_specs=[vmem, vmem],
        out_specs=(vmem, vmem),
    )(found, sums)


def solution(mesh):
    D, S = mesh.shape["dict"], mesh.shape["scan"]
    return jax.shard_map(
        functools.partial(shards, D, S),
        mesh=mesh,
        in_specs=(
            P("scan", "dict", None),
            P(),
            P("dict", None),
            P("scan", "dict"),
            P("scan", "dict"),
            P(),
        ),
        out_specs=(P("scan", "dict"), P("scan", None)),
        check_vma=False,
    )
```

```python
import functools

import jax
import jax.numpy as jnp
from jax import lax
from jax.experimental import pallas as pl
from jax.experimental.pallas import tpu as pltpu
from jax.sharding import PartitionSpec as P

MESH = pl.DeviceIdType.MESH
EPS = 1e-05
GROUP = 8
F32 = jnp.float32
BF16 = jnp.bfloat16


def iota(shape, dim):
    return lax.broadcasted_iota(jnp.int32, shape, dim)


def near(a, b):
    return (a - b <= 1) & (b - a <= 1)


def unit(values, pixels):
    square = jnp.sum(values * values, axis=-1, keepdims=True) * (1.0 / pixels)
    return values * lax.rsqrt(square + EPS)


def centred(values, pixels):
    return values - jnp.sum(values, axis=-1, keepdims=True) * (1.0 / pixels)


def kernel(
    D, S, G, TR, TC, pix, R,
    patterns, templates, background, grain_id, keep_mask, grain_row,
    score_out, grain_out,
    pat, raw, ground, filt, near_mat, halo_mat, sel_mat,
    edge_rows, edge, corner_src, corner_dst, halo, neigh, indexed, panel,
    gsum, grecv, zbuf, best,
    pat_sem, raw_sem, ground_sem, zsend, nsend, trecv, hsend, hrecv,
    gsend, grecv_sem, zgsend, zgrecv,
):
    z = lax.axis_index("dict")
    s = lax.axis_index("scan")
    points = TR * TC
    rows_out = G // S
    run = panel.shape[2]
    wide_pix = run * GROUP
    cuts = [(a, min(a + 512, pix)) for a in range(0, pix, 512)]

    def pat_copy(i):
        return pltpu.make_async_copy(patterns.at[i], pat.at[i], pat_sem.at[i])

    raw_copy = pltpu.make_async_copy(templates, raw, raw_sem)
    raw_copy.start()
    ground_copy = pltpu.make_async_copy(background, ground.at[0], ground_sem)
    ground_copy.start()
    for i in [TR - 1] + list(range(TR - 1)):
        pat_copy(i).start()

    halo[...] = jnp.zeros_like(halo)
    tail = pix // 128 * 128
    indexed[:, tail:] = jnp.zeros((points, wide_pix - tail), BF16)

    barrier = pltpu.get_barrier_semaphore()

    def hello(zz, ss):
        pl.semaphore_signal(
            barrier, inc=1, device_id={"dict": zz, "scan": ss}, device_id_type=MESH
        )

    for k in range(1, S):
        hello(z, lax.rem(s + k, S))
    for k in range(1, D):
        hello(lax.rem(z + k, D), s)
    diagonals = [(-1, -1), (-1, 1), (1, -1), (1, 1)]

    def inside(ds, dz):
        ok = None
        for cond in (
            [s >= 1] if ds < 0 else [s <= S - 2] if ds > 0 else []
        ) + ([z >= 1] if dz < 0 else [z <= D - 2] if dz > 0 else []):
            ok = cond if ok is None else ok & cond
        return ok

    for ds, dz in diagonals:
        @pl.when(inside(ds, dz))
        def _():
            hello(z + dz, s + ds)

    bits, low = TC.bit_length() - 1, TC - 1
    p0, q1 = iota((points, points), 0), iota((points, points), 1)
    near_mat[...] = jnp.where(
        near(p0 >> bits, q1 >> bits) & near(p0 & low, q1 & low), 1.0, 0.0
    ).astype(BF16)
    p, h = iota((points, 128), 0), iota((points, 128), 1)
    slot, i = h >> 4, h & 15
    r, c = p >> bits, p & low
    side = (
        ((slot == 0) & (r == 0) & near(c, i))
        | ((slot == 1) & (r == TR - 1) & near(c, i))
        | ((slot == 2) & (c == 0) & near(r, i))
        | ((slot == 3) & (c == TC - 1) & near(r, i))
        | ((slot == 4) & (i == 0) & (p == 0))
        | ((slot == 5) & (i == 0) & (p == TC - 1))
        | ((slot == 6) & (i == 0) & (p == points - TC))
        | ((slot == 7) & (i == 0) & (p == points - 1))
    )
    halo_mat[...] = jnp.where(side, 1.0, 0.0).astype(BF16)
    code = jnp.where(keep_mask[...] == 1, grain_id[...], -1).astype(F32).astype(BF16)
    spread = jnp.where((iota((TC, points), 1) & low) == iota((TC, points), 0), 1.0, 0.0).astype(BF16)
    wide = jnp.dot(code, spread, preferred_element_type=F32)
    own = (iota((TR, points), 1) >> bits) == iota((TR, points), 0)
    code_row = jnp.sum(jnp.where(own, wide, 0.0), axis=0, keepdims=True)
    one_hot = jnp.where(
        iota((G, points), 0).astype(F32) == code_row, 1.0, 0.0
    ).astype(BF16)
    to_row = jnp.where(iota((G, G), 0) == grain_row[...], 1.0, 0.0).astype(BF16)
    sel_mat[...] = jnp.dot(to_row, one_hot, preferred_element_type=F32).astype(BF16)

    in_group = lax.rem(s, GROUP)
    base = s - in_group
    core = lax.rem(in_group, 2)
    chip = in_group // 2
    xbit = lax.rem(chip, 2)
    ybit = chip // 2
    piece = core * 4 + chip
    px, py = piece + 1 - 2 * xbit, piece + 2 - 4 * ybit
    first = jnp.where(core == 0, px, py)
    second = jnp.where(core == 0, py, px)
    across = first + second - piece
    twin = piece + 4 - 8 * core

    def holder(q):
        return base + lax.rem(q, 4) * 2 + q // 4

    def remote(src, dst, ssem, rsem, zz, ss):
        return pltpu.make_async_remote_copy(
            src_ref=src, dst_ref=dst, send_sem=ssem, recv_sem=rsem,
            device_id={"dict": zz, "scan": ss}, device_id_type=MESH,
        )

    def shard_copy(d, q, ssem, zz, ss):
        return remote(panel.at[d, q], panel.at[d, q], ssem, trecv.at[d, q], zz, ss)

    def z_copy(d, k, zz):
        return shard_copy(d, piece, zsend.at[k], zz, s)

    def z_both(act):
        for k, step in ((z, 1), (D, -1)):
            @pl.when((z + step >= 0) & (z + step < D))
            def _():
                act(z_copy(z, k, z + step))

    def normalise():
        mean = jnp.sum(raw[...].astype(F32), axis=0, keepdims=True) * (1.0 / pix)
        off = raw[...].astype(F32) - mean
        square = jnp.sum(off * off, axis=0, keepdims=True) * (1.0 / pix)
        gain = lax.rsqrt(square + EPS)
        for j in range(GROUP):
            a, b = j * run, min((j + 1) * run, pix)
            panel[z, j, 0 : b - a, :] = ((raw[a:b, :].astype(F32) - mean) * gain).astype(BF16)
            if b - a < run:
                panel[z, j, b - a : run, :] = jnp.zeros((run - b + a, R), BF16)

    near_end = jnp.minimum(z, D - 1 - z)

    def event_shard(e):
        paired = e <= 2 * near_end
        k = jnp.where(paired, (e + 1) // 2, e - near_end)
        lower = jnp.where(paired, e % 2 == 1, z > near_end)
        return jnp.where(lower, z - k, z + k)

    def relay(d, act):
        target = jnp.where(d < z, z + 1, z - 1)

        @pl.when((target >= 0) & (target < D))
        def _():
            act(z_copy(d, d, target))

    def in_plane(d, k):
        q, to = ((piece, first), (piece, second), (first, second))[k]
        return shard_copy(d, q, nsend.at[d, k], z, holder(to))

    def core_copy(d, core):
        four = panel.at[d, pl.ds(core * 4, 4)]
        return remote(four, four, nsend.at[d, 3], trecv.at[d, core * 4], z, holder(twin))

    def arrived(d, q):
        shard_copy(d, q, nsend.at[d, 0], z, holder(first)).wait_recv()

    def stage_a(e):
        d = event_shard(e)
        arrived(d, piece)
        relay(d, lambda copy: copy.start())
        in_plane(d, 0).start()
        in_plane(d, 1).start()

    def stage_b(e):
        d = event_shard(e)
        arrived(d, first)
        in_plane(d, 2).start()

    def stage_c(e):
        d = event_shard(e)
        arrived(d, second)
        arrived(d, across)
        core_copy(d, core).start()

    def score(d):
        dots = jnp.dot(
            indexed[...], panel[d].reshape(wide_pix, R), preferred_element_type=F32
        )
        best[...] = jnp.maximum(best[...], dots)

    def stage_d(e):
        d = event_shard(e)
        core_copy(d, 1 - core).wait_recv()
        score(d)

    def stage_end(e):
        d = event_shard(e)
        relay(d, lambda copy: copy.wait_send())
        for k in range(3):
            in_plane(d, k).wait_send()
        core_copy(d, core).wait_send()

    halo_moves = [
        (filt.at[TR - 1], halo.at[0], 1, 0),
        (filt.at[0], halo.at[1], -1, 0),
        (edge.at[1], halo.at[2], 0, 1),
        (edge.at[0], halo.at[3], 0, -1),
        (corner_src.at[3], corner_dst.at[0], 1, 1),
        (corner_src.at[2], corner_dst.at[1], 1, -1),
        (corner_src.at[1], corner_dst.at[2], -1, 1),
        (corner_src.at[0], corner_dst.at[3], -1, -1),
    ]

    def halo_copy(k):
        src, dst, ds, dz = halo_moves[k]
        return remote(src, dst, hsend.at[k], hrecv.at[k], z + dz, s + ds)

    def halo_send(k):
        @pl.when(inside(halo_moves[k][2], halo_moves[k][3]))
        def _():
            halo_copy(k).start()

    diag_count = sum(
        [jnp.where(inside(ds, dz), 1, 0) for ds, dz in diagonals]
    )
    raw_copy.wait()
    normalise()
    pl.semaphore_wait(barrier, S - 1 + D - 1 + diag_count)


    z_both(lambda copy: copy.start())

    def filter_rows(a, b):
        for i in range(a, b):
            pat_copy(i).wait()
        centre = centred(pat[a:b] - ground[...].reshape(1, 1, pix), pix)
        values = unit(centre, pix)
        filt[a:b] = values.astype(BF16)
        for i in range(a, b):
            edge_rows[0, i : i + 1, :] = values[i - a, 0:1, :]
            edge_rows[1, i : i + 1, :] = values[i - a, TC - 1 : TC, :]

    ground_copy.wait()
    filter_rows(TR - 1, TR)
    filter_rows(0, 1)
    halo_send(0)
    halo_send(1)
    for a in range(1, TR - 1, 7):
        filter_rows(a, min(a + 7, TR - 1))
    edge[...] = edge_rows[...].astype(BF16)
    for k, (side, i) in enumerate([(0, 0), (1, 0), (0, TR - 1), (1, TR - 1)]):
        corner_src[k] = jnp.broadcast_to(edge_rows[side, i : i + 1, :], (2, pix)).astype(BF16)
    for k in range(2, 8):
        halo_send(k)

    events = min(D - 1, 3)
    stage_a(1)
    if events >= 3:
        @pl.when(near_end > 0)
        def _():
            stage_a(2)

    for a, b in cuts:
        neigh[:, a:b] = jnp.dot(
            near_mat[...], filt[:, :, a:b].reshape(points, b - a), preferred_element_type=F32
        )
    stage_b(1)
    if events >= 3:
        @pl.when(near_end > 0)
        def _():
            stage_b(2)
            stage_a(3)

        @pl.when(near_end == 0)
        def _():
            stage_a(2)
    elif events >= 2:
        stage_a(2)

    for k in range(8):
        ds, dz = halo_moves[k][2], halo_moves[k][3]

        @pl.when(inside(-ds, -dz))
        def _():
            halo_copy(k).wait_recv()
            if k >= 4:
                halo[k, 0:2, :] = corner_dst[k - 4]

    total = jnp.zeros((points, 1), F32)
    for a, b in cuts:
        part = neigh[:, a:b] + jnp.dot(
            halo_mat[...], halo[:, :, a:b].reshape(128, b - a), preferred_element_type=F32
        )
        neigh[:, a:b] = part
        total = total + jnp.sum(part * part, axis=1, keepdims=True)
    scale = lax.rsqrt(total * (1.0 / pix) + EPS)
    for a, b in cuts:
        indexed[:, a:b] = (neigh[:, a:b] * scale).astype(BF16)

    for a, b in cuts:
        sums = jnp.dot(sel_mat[...], indexed[:, a:b], preferred_element_type=F32).astype(BF16)
        for k in range(S):
            gsum[k, :, a:b] = sums[k * rows_out : (k + 1) * rows_out]

    def grain_copy(to):
        return remote(gsum.at[to], grecv.at[s], gsend.at[to], grecv_sem.at[s], z, to)

    for k in range(1, S):
        grain_copy(lax.rem(s + k, S)).start()

    stage_c(1)
    if events >= 3:
        @pl.when(near_end == 0)
        def _():
            stage_b(2)
            stage_a(3)

        @pl.when(near_end > 0)
        def _():
            stage_c(2)
            stage_b(3)
    elif events >= 2:
        stage_b(2)
    best[...] = jnp.full_like(best, -1e30)
    score(z)

    for k in range(1, S):
        source = lax.rem(s + k, S)
        remote(
            gsum.at[source], grecv.at[source], gsend.at[source], grecv_sem.at[source], z, source
        ).wait_recv()
    grecv[s] = gsum[s]
    held = jnp.zeros((rows_out, pix), F32)
    for k in range(S):
        held = held + grecv[k].astype(F32)
    zbuf[z] = held.astype(BF16)

    def z_grain(to, at):
        return remote(zbuf.at[at], zbuf.at[at], zgsend.at[to], zgrecv.at[at], to, s)

    for k in range(1, D):
        z_grain(lax.rem(z + k, D), z).start()

    stage_d(1)
    if events >= 3:
        @pl.when(near_end == 0)
        def _():
            stage_c(2)
            stage_b(3)
    elif events >= 2:
        stage_c(2)
    if events >= 2:
        stage_d(2)
    if events >= 3:
        stage_c(3)

    for k in range(1, D):
        source = lax.rem(z + k, D)
        z_grain(source, source).wait_recv()
    held = jnp.zeros((rows_out, pix), F32)
    for k in range(D):
        held = held + zbuf[k].astype(F32)
    grain_out[...] = unit(held, pix)

    if events >= 3:
        stage_d(3)
    if D > 4:
        @pl.loop(4, D)
        def _(e):
            stage_a(e)
            stage_b(e)
            stage_c(e)
            stage_d(e)

    score_row = jnp.max(best[...].T, axis=0, keepdims=True) * (1.0 / pix**0.5)
    for k in range(TR):
        score_out[k : k + 1, :] = score_row[:, k * TC : (k + 1) * TC]

    z_both(lambda copy: copy.wait_send())

    @pl.loop(1, D)
    def _(e):
        stage_end(e)

    for k in range(8):
        @pl.when(inside(halo_moves[k][2], halo_moves[k][3]))
        def _():
            halo_copy(k).wait_send()

    for k in range(1, S):
        grain_copy(lax.rem(s + k, S)).wait_send()
    for k in range(1, D):
        z_grain(lax.rem(z + k, D), z).wait_send()


def hand_over(found, sums, score_out, grain_out):
    score_out[...] = found[...]
    grain_out[...] = sums[...]


def shards(D, S, patterns, background, templates, grain_id, keep_mask, grain_row):
    TR, TC, pix = patterns.shape
    R = templates.shape[0]
    G = grain_row.shape[0]
    rows_out = G // S
    points = TR * TC
    run = -(-pix // (GROUP * 16)) * 16
    dma = pltpu.SemaphoreType.DMA
    vmem = pl.BlockSpec(memory_space=pltpu.VMEM)
    anywhere = pl.BlockSpec(memory_space=pl.ANY)
    found, sums = pl.pallas_call(
        functools.partial(kernel, D, S, G, TR, TC, pix, R),
        out_shape=(
            jax.ShapeDtypeStruct((TR, TC), F32),
            jax.ShapeDtypeStruct((rows_out, pix), F32),
        ),
        in_specs=[anywhere, anywhere, anywhere, vmem, vmem, vmem],
        out_specs=(vmem, vmem),
        scratch_shapes=[
            pltpu.VMEM((TR, TC, pix), F32),
            pltpu.VMEM((pix, R), BF16),
            pltpu.VMEM((1, pix), F32),
            pltpu.VMEM((TR, TC, pix), BF16),
            pltpu.VMEM((points, points), BF16),
            pltpu.VMEM((points, 128), BF16),
            pltpu.VMEM((G, points), BF16),
            pltpu.VMEM((2, 16, pix), F32),
            pltpu.VMEM((2, 16, pix), BF16),
            pltpu.VMEM((4, 2, pix), BF16),
            pltpu.VMEM((4, 2, pix), BF16),
            pltpu.VMEM((8, 16, pix), BF16),
            pltpu.VMEM((points, pix), F32),
            pltpu.VMEM((points, run * GROUP), BF16),
            pltpu.VMEM((D, GROUP, run, R), BF16),
            pltpu.VMEM((S, rows_out, pix), BF16),
            pltpu.VMEM((S, rows_out, pix), BF16),
            pltpu.VMEM((D, rows_out, pix), BF16),
            pltpu.VMEM((points, R), F32),
            dma((TR,)),
            dma,
            dma,
            dma((D + 1,)),
            dma((D, 4)),
            dma((D, GROUP)),
            dma((8,)),
            dma((8,)),
            dma((S,)),
            dma((S,)),
            dma((D,)),
            dma((D,)),
        ],
        compiler_params=pltpu.CompilerParams(
            collective_id=0, has_side_effects=True, vmem_limit_bytes=56 * 1024 * 1024
        ),
    )(
        patterns,
        templates.T,
        background,
        grain_id,
        keep_mask,
        grain_row.reshape(1, G),
    )
    return pl.pallas_call(
        hand_over,
        out_shape=(
            jax.ShapeDtypeStruct(found.shape, F32),
            jax.ShapeDtypeStruct(sums.shape, F32),
        ),
        in_specs=[vmem, vmem],
        out_specs=(vmem, vmem),
    )(found, sums)


def solution(mesh):
    D, S = mesh.shape["dict"], mesh.shape["scan"]
    return jax.shard_map(
        functools.partial(shards, D, S),
        mesh=mesh,
        in_specs=(
            P("scan", "dict", None),
            P(),
            P("dict", None),
            P("scan", "dict"),
            P("scan", "dict"),
            P(),
        ),
        out_specs=(P("scan", "dict"), P("scan", None)),
        check_vma=False,
    )
```

```python
import functools

import jax
import jax.numpy as jnp
from jax import lax
from jax.experimental import pallas as pl
from jax.experimental.pallas import tpu as pltpu
from jax.sharding import PartitionSpec as P

MESH = pl.DeviceIdType.MESH
EPS = 1e-05
GROUP = 8
F32 = jnp.float32
BF16 = jnp.bfloat16


def iota(shape, dim):
    return lax.broadcasted_iota(jnp.int32, shape, dim)


def near(a, b):
    return (a - b <= 1) & (b - a <= 1)


def unit(values, pixels):
    square = jnp.sum(values * values, axis=-1, keepdims=True) * (1.0 / pixels)
    return values * lax.rsqrt(square + EPS)


def centred(values, pixels):
    return values - jnp.sum(values, axis=-1, keepdims=True) * (1.0 / pixels)


def kernel(
    D, S, G, TR, TC, pix, R,
    patterns, templates, background, grain_id, keep_mask, grain_row,
    score_out, grain_out,
    pat, raw, ground, filt, near_mat, halo_mat, sel_mat,
    edge_rows, edge, corner_src, corner_dst, halo, neigh, indexed, panel,
    gsum, grecv, zbuf, best,
    pat_sem, raw_sem, ground_sem, zsend, nsend, trecv, hsend, hrecv,
    gsend, grecv_sem, zgsend, zgrecv,
):
    z = lax.axis_index("dict")
    s = lax.axis_index("scan")
    points = TR * TC
    rows_out = G // S
    run = panel.shape[2]
    wide_pix = run * GROUP
    cuts = [(a, min(a + 512, pix)) for a in range(0, pix, 512)]

    def pat_copy(i):
        return pltpu.make_async_copy(patterns.at[i], pat.at[i], pat_sem.at[i])

    raw_copy = pltpu.make_async_copy(templates, raw, raw_sem)
    raw_copy.start()
    ground_copy = pltpu.make_async_copy(background, ground.at[0], ground_sem)
    ground_copy.start()
    for i in [TR - 1] + list(range(TR - 1)):
        pat_copy(i).start()

    halo[...] = jnp.zeros_like(halo)
    tail = pix // 128 * 128
    indexed[:, tail:] = jnp.zeros((points, wide_pix - tail), BF16)

    barrier = pltpu.get_barrier_semaphore()

    def hello(zz, ss):
        pl.semaphore_signal(
            barrier, inc=1, device_id={"dict": zz, "scan": ss}, device_id_type=MESH
        )

    for k in range(1, S):
        hello(z, lax.rem(s + k, S))
    for k in range(1, D):
        hello(lax.rem(z + k, D), s)
    diagonals = [(-1, -1), (-1, 1), (1, -1), (1, 1)]

    def inside(ds, dz):
        ok = None
        for cond in (
            [s >= 1] if ds < 0 else [s <= S - 2] if ds > 0 else []
        ) + ([z >= 1] if dz < 0 else [z <= D - 2] if dz > 0 else []):
            ok = cond if ok is None else ok & cond
        return ok

    for ds, dz in diagonals:
        @pl.when(inside(ds, dz))
        def _():
            hello(z + dz, s + ds)

    bits, low = TC.bit_length() - 1, TC - 1
    p0, q1 = iota((points, points), 0), iota((points, points), 1)
    near_mat[...] = jnp.where(
        near(p0 >> bits, q1 >> bits) & near(p0 & low, q1 & low), 1.0, 0.0
    ).astype(BF16)
    p, h = iota((points, 128), 0), iota((points, 128), 1)
    slot, i = h >> 4, h & 15
    r, c = p >> bits, p & low
    side = (
        ((slot == 0) & (r == 0) & near(c, i))
        | ((slot == 1) & (r == TR - 1) & near(c, i))
        | ((slot == 2) & (c == 0) & near(r, i))
        | ((slot == 3) & (c == TC - 1) & near(r, i))
        | ((slot == 4) & (i == 0) & (p == 0))
        | ((slot == 5) & (i == 0) & (p == TC - 1))
        | ((slot == 6) & (i == 0) & (p == points - TC))
        | ((slot == 7) & (i == 0) & (p == points - 1))
    )
    halo_mat[...] = jnp.where(side, 1.0, 0.0).astype(BF16)
    code = jnp.where(keep_mask[...] == 1, grain_id[...], -1).astype(F32).astype(BF16)
    spread = jnp.where((iota((TC, points), 1) & low) == iota((TC, points), 0), 1.0, 0.0).astype(BF16)
    wide = jnp.dot(code, spread, preferred_element_type=F32)
    own = (iota((TR, points), 1) >> bits) == iota((TR, points), 0)
    code_row = jnp.sum(jnp.where(own, wide, 0.0), axis=0, keepdims=True)
    one_hot = jnp.where(
        iota((G, points), 0).astype(F32) == code_row, 1.0, 0.0
    ).astype(BF16)
    to_row = jnp.where(iota((G, G), 0) == grain_row[...], 1.0, 0.0).astype(BF16)
    sel_mat[...] = jnp.dot(to_row, one_hot, preferred_element_type=F32).astype(BF16)

    in_group = lax.rem(s, GROUP)
    base = s - in_group
    core = lax.rem(in_group, 2)
    chip = in_group // 2
    xbit = lax.rem(chip, 2)
    ybit = chip // 2
    piece = core * 4 + chip
    px, py = piece + 1 - 2 * xbit, piece + 2 - 4 * ybit
    first = jnp.where(core == 0, px, py)
    second = jnp.where(core == 0, py, px)
    across = first + second - piece
    twin = piece + 4 - 8 * core

    def holder(q):
        return base + lax.rem(q, 4) * 2 + q // 4

    def remote(src, dst, ssem, rsem, zz, ss):
        return pltpu.make_async_remote_copy(
            src_ref=src, dst_ref=dst, send_sem=ssem, recv_sem=rsem,
            device_id={"dict": zz, "scan": ss}, device_id_type=MESH,
        )

    half = run // 32 * 16
    halves = ((0, 0, run - half), (1, run - half, half))

    def shard_copy(d, q, part, ssem, zz, ss):
        h, at, size = part
        rows = panel.at[d, q, pl.ds(at, size)]
        return remote(rows, rows, ssem, trecv.at[d, q, h], zz, ss)

    def z_copy(d, k, part, zz):
        return shard_copy(d, piece, part, zsend.at[k, part[0]], zz, s)

    def z_both(act):
        for part in halves:
            for k, step in ((z, 1), (D, -1)):
                @pl.when((z + step >= 0) & (z + step < D))
                def _():
                    act(z_copy(z, k, part, z + step))

    def normalise():
        mean = jnp.sum(raw[...].astype(F32), axis=0, keepdims=True) * (1.0 / pix)
        off = raw[...].astype(F32) - mean
        square = jnp.sum(off * off, axis=0, keepdims=True) * (1.0 / pix)
        gain = lax.rsqrt(square + EPS)
        for j in range(GROUP):
            a, b = j * run, min((j + 1) * run, pix)
            panel[z, j, 0 : b - a, :] = ((raw[a:b, :].astype(F32) - mean) * gain).astype(BF16)
            if b - a < run:
                panel[z, j, b - a : run, :] = jnp.zeros((run - b + a, R), BF16)

    near_end = jnp.minimum(z, D - 1 - z)

    def event_shard(e):
        paired = e <= 2 * near_end
        k = jnp.where(paired, (e + 1) // 2, e - near_end)
        lower = jnp.where(paired, e % 2 == 1, z > near_end)
        return jnp.where(lower, z - k, z + k)

    def relay(d, part, act):
        target = jnp.where(d < z, z + 1, z - 1)

        @pl.when((target >= 0) & (target < D))
        def _():
            act(z_copy(d, d, part, target))

    def in_plane(d, k, part):
        q, to = ((piece, first), (piece, second), (first, second))[k]
        return shard_copy(d, q, part, nsend.at[d, k, part[0]], z, holder(to))

    def core_copy(d, core):
        four = panel.at[d, pl.ds(core * 4, 4)]
        return remote(four, four, nsend.at[d, 3, 0], trecv.at[d, core * 4, 0], z, holder(twin))

    def arrived(d, q, part):
        shard_copy(d, q, part, nsend.at[d, 0, 0], z, holder(first)).wait_recv()

    def stage_a(e):
        d = event_shard(e)
        for part in halves:
            arrived(d, piece, part)
            relay(d, part, lambda copy: copy.start())
            in_plane(d, 0, part).start()
            in_plane(d, 1, part).start()

    def stage_b(e):
        d = event_shard(e)
        for part in halves:
            arrived(d, first, part)
            in_plane(d, 2, part).start()

    def stage_c(e):
        d = event_shard(e)
        for part in halves:
            arrived(d, second, part)
            arrived(d, across, part)
        core_copy(d, core).start()

    def score(d):
        dots = jnp.dot(
            indexed[...], panel[d].reshape(wide_pix, R), preferred_element_type=F32
        )
        best[...] = jnp.maximum(best[...], dots)

    def stage_d(e):
        d = event_shard(e)
        core_copy(d, 1 - core).wait_recv()
        score(d)

    def stage_end(e):
        d = event_shard(e)
        for part in halves:
            relay(d, part, lambda copy: copy.wait_send())
            for k in range(3):
                in_plane(d, k, part).wait_send()
        core_copy(d, core).wait_send()

    halo_moves = [
        (filt.at[TR - 1], halo.at[0], 1, 0),
        (filt.at[0], halo.at[1], -1, 0),
        (edge.at[1], halo.at[2], 0, 1),
        (edge.at[0], halo.at[3], 0, -1),
        (corner_src.at[3], corner_dst.at[0], 1, 1),
        (corner_src.at[2], corner_dst.at[1], 1, -1),
        (corner_src.at[1], corner_dst.at[2], -1, 1),
        (corner_src.at[0], corner_dst.at[3], -1, -1),
    ]

    def halo_copy(k):
        src, dst, ds, dz = halo_moves[k]
        return remote(src, dst, hsend.at[k], hrecv.at[k], z + dz, s + ds)

    def halo_send(k):
        @pl.when(inside(halo_moves[k][2], halo_moves[k][3]))
        def _():
            halo_copy(k).start()

    diag_count = sum(
        [jnp.where(inside(ds, dz), 1, 0) for ds, dz in diagonals]
    )
    raw_copy.wait()
    normalise()
    pl.semaphore_wait(barrier, S - 1 + D - 1 + diag_count)


    z_both(lambda copy: copy.start())

    def filter_rows(a, b):
        for i in range(a, b):
            pat_copy(i).wait()
        centre = centred(pat[a:b] - ground[...].reshape(1, 1, pix), pix)
        values = unit(centre, pix)
        filt[a:b] = values.astype(BF16)
        for i in range(a, b):
            edge_rows[0, i : i + 1, :] = values[i - a, 0:1, :]
            edge_rows[1, i : i + 1, :] = values[i - a, TC - 1 : TC, :]

    ground_copy.wait()
    filter_rows(TR - 1, TR)
    filter_rows(0, 1)
    halo_send(0)
    halo_send(1)
    for a in range(1, TR - 1, 7):
        filter_rows(a, min(a + 7, TR - 1))
    edge[...] = edge_rows[...].astype(BF16)
    for k, (side, i) in enumerate([(0, 0), (1, 0), (0, TR - 1), (1, TR - 1)]):
        corner_src[k] = jnp.broadcast_to(edge_rows[side, i : i + 1, :], (2, pix)).astype(BF16)
    for k in range(2, 8):
        halo_send(k)

    events = min(D - 1, 3)
    stage_a(1)
    if events >= 3:
        @pl.when(near_end > 0)
        def _():
            stage_a(2)

    for a, b in cuts:
        neigh[:, a:b] = jnp.dot(
            near_mat[...], filt[:, :, a:b].reshape(points, b - a), preferred_element_type=F32
        )
    stage_b(1)
    if events >= 3:
        @pl.when(near_end > 0)
        def _():
            stage_b(2)
            stage_a(3)

        @pl.when(near_end == 0)
        def _():
            stage_a(2)
    elif events >= 2:
        stage_a(2)

    for k in range(8):
        ds, dz = halo_moves[k][2], halo_moves[k][3]

        @pl.when(inside(-ds, -dz))
        def _():
            halo_copy(k).wait_recv()
            if k >= 4:
                halo[k, 0:2, :] = corner_dst[k - 4]

    total = jnp.zeros((points, 1), F32)
    for a, b in cuts:
        part = neigh[:, a:b] + jnp.dot(
            halo_mat[...], halo[:, :, a:b].reshape(128, b - a), preferred_element_type=F32
        )
        neigh[:, a:b] = part
        total = total + jnp.sum(part * part, axis=1, keepdims=True)
    scale = lax.rsqrt(total * (1.0 / pix) + EPS)
    for a, b in cuts:
        indexed[:, a:b] = (neigh[:, a:b] * scale).astype(BF16)

    for a, b in cuts:
        sums = jnp.dot(sel_mat[...], indexed[:, a:b], preferred_element_type=F32).astype(BF16)
        for k in range(S):
            gsum[k, :, a:b] = sums[k * rows_out : (k + 1) * rows_out]

    def grain_copy(to):
        return remote(gsum.at[to], grecv.at[s], gsend.at[to], grecv_sem.at[s], z, to)

    for k in range(1, S):
        grain_copy(lax.rem(s + k, S)).start()

    stage_c(1)
    if events >= 3:
        @pl.when(near_end == 0)
        def _():
            stage_b(2)

        @pl.when(near_end > 0)
        def _():
            stage_c(2)
            stage_b(3)
    elif events >= 2:
        stage_b(2)
    best[...] = jnp.full_like(best, -1e30)
    score(z)
    stage_d(1)
    if events >= 3:
        @pl.when(near_end == 0)
        def _():
            stage_a(3)

    for k in range(1, S):
        source = lax.rem(s + k, S)
        remote(
            gsum.at[source], grecv.at[source], gsend.at[source], grecv_sem.at[source], z, source
        ).wait_recv()
    grecv[s] = gsum[s]
    held = jnp.zeros((rows_out, pix), F32)
    for k in range(S):
        held = held + grecv[k].astype(F32)
    zbuf[z] = held.astype(BF16)

    def z_grain(to, at):
        return remote(zbuf.at[at], zbuf.at[at], zgsend.at[to], zgrecv.at[at], to, s)

    for k in range(1, D):
        z_grain(lax.rem(z + k, D), z).start()

    if events >= 3:
        @pl.when(near_end == 0)
        def _():
            stage_c(2)
            stage_b(3)
    elif events >= 2:
        stage_c(2)
    if events >= 2:
        stage_d(2)
    if events >= 3:
        stage_c(3)

    for k in range(1, D):
        source = lax.rem(z + k, D)
        z_grain(source, source).wait_recv()
    held = jnp.zeros((rows_out, pix), F32)
    for k in range(D):
        held = held + zbuf[k].astype(F32)
    grain_out[...] = unit(held, pix)

    if events >= 3:
        stage_d(3)
    if D > 4:
        @pl.loop(4, D)
        def _(e):
            stage_a(e)
            stage_b(e)
            stage_c(e)
            stage_d(e)

    score_row = jnp.max(best[...].T, axis=0, keepdims=True) * (1.0 / pix**0.5)
    for k in range(TR):
        score_out[k : k + 1, :] = score_row[:, k * TC : (k + 1) * TC]

    z_both(lambda copy: copy.wait_send())

    @pl.loop(1, D)
    def _(e):
        stage_end(e)

    for k in range(8):
        @pl.when(inside(halo_moves[k][2], halo_moves[k][3]))
        def _():
            halo_copy(k).wait_send()

    for k in range(1, S):
        grain_copy(lax.rem(s + k, S)).wait_send()
    for k in range(1, D):
        z_grain(lax.rem(z + k, D), z).wait_send()


def hand_over(found, sums, score_out, grain_out):
    score_out[...] = found[...]
    grain_out[...] = sums[...]


def shards(D, S, patterns, background, templates, grain_id, keep_mask, grain_row):
    TR, TC, pix = patterns.shape
    R = templates.shape[0]
    G = grain_row.shape[0]
    rows_out = G // S
    points = TR * TC
    run = -(-pix // (GROUP * 16)) * 16
    dma = pltpu.SemaphoreType.DMA
    vmem = pl.BlockSpec(memory_space=pltpu.VMEM)
    anywhere = pl.BlockSpec(memory_space=pl.ANY)
    found, sums = pl.pallas_call(
        functools.partial(kernel, D, S, G, TR, TC, pix, R),
        out_shape=(
            jax.ShapeDtypeStruct((TR, TC), F32),
            jax.ShapeDtypeStruct((rows_out, pix), F32),
        ),
        in_specs=[anywhere, anywhere, anywhere, vmem, vmem, vmem],
        out_specs=(vmem, vmem),
        scratch_shapes=[
            pltpu.VMEM((TR, TC, pix), F32),
            pltpu.VMEM((pix, R), BF16),
            pltpu.VMEM((1, pix), F32),
            pltpu.VMEM((TR, TC, pix), BF16),
            pltpu.VMEM((points, points), BF16),
            pltpu.VMEM((points, 128), BF16),
            pltpu.VMEM((G, points), BF16),
            pltpu.VMEM((2, 16, pix), F32),
            pltpu.VMEM((2, 16, pix), BF16),
            pltpu.VMEM((4, 2, pix), BF16),
            pltpu.VMEM((4, 2, pix), BF16),
            pltpu.VMEM((8, 16, pix), BF16),
            pltpu.VMEM((points, pix), F32),
            pltpu.VMEM((points, run * GROUP), BF16),
            pltpu.VMEM((D, GROUP, run, R), BF16),
            pltpu.VMEM((S, rows_out, pix), BF16),
            pltpu.VMEM((S, rows_out, pix), BF16),
            pltpu.VMEM((D, rows_out, pix), BF16),
            pltpu.VMEM((points, R), F32),
            dma((TR,)),
            dma,
            dma,
            dma((D + 1, 2)),
            dma((D, 4, 2)),
            dma((D, GROUP, 2)),
            dma((8,)),
            dma((8,)),
            dma((S,)),
            dma((S,)),
            dma((D,)),
            dma((D,)),
        ],
        compiler_params=pltpu.CompilerParams(
            collective_id=0, has_side_effects=True, vmem_limit_bytes=56 * 1024 * 1024
        ),
    )(
        patterns,
        templates.T,
        background,
        grain_id,
        keep_mask,
        grain_row.reshape(1, G),
    )
    return pl.pallas_call(
        hand_over,
        out_shape=(
            jax.ShapeDtypeStruct(found.shape, F32),
            jax.ShapeDtypeStruct(sums.shape, F32),
        ),
        in_specs=[vmem, vmem],
        out_specs=(vmem, vmem),
    )(found, sums)


def solution(mesh):
    D, S = mesh.shape["dict"], mesh.shape["scan"]
    return jax.shard_map(
        functools.partial(shards, D, S),
        mesh=mesh,
        in_specs=(
            P("scan", "dict", None),
            P(),
            P("dict", None),
            P("scan", "dict"),
            P("scan", "dict"),
            P(),
        ),
        out_specs=(P("scan", "dict"), P("scan", None)),
        check_vma=False,
    )
```
